256 devices in a mesh: dp: 64 (over z, y, core), rep: 4 (over x).
Axes of the slice: x: 4, y: 4, z: 8, core: 2. Of those that a mesh axis runs over, the one named last changes fastest.
Arguments:
- waveform: bfloat16 [4, 3072, 320], P('rep', 'dp'), may hold values from -6 to 6
- lengths: int32 [4, 3072], P('rep', 'dp'), may hold values from 214 to 320
- target: int32 [4, 3072], P('rep', 'dp'), may hold values from 0 to 3071, as said below
- conv0_weight: bfloat16 [10, 512], replicated, may hold values from -2 to 2
- norm_gain: float32 [512], replicated, may hold values from 0.5 to 1.5
- norm_bias: float32 [512], replicated, may hold values from -0.5 to 0.5
- conv1_weight: bfloat16 [3, 512, 512], replicated, may hold values from -0.15625 to 0.15625
- feature_grad: bfloat16 [4, 3072, 31, 512], P('rep', 'dp'), may hold values from -6 to 6
Outputs:
- features: bfloat16 [4, 3072, 31, 512], P('rep', 'dp')
- grad_conv0: float32 [10, 512], replicated
- grad_gain: float32 [512], replicated
- grad_bias: float32 [512], replicated
- grad_conv1: float32 [3, 512, 512], replicated
The draws below stay inside these ranges and needn't reach their ends.
Inputs may be any that keep to these rules, and one draw needn't show every extreme that they name: In each group target is a permutation of the 3072 slots; the spans of one device go to slots of devices along dp such that every pair of devices exchanges either 0 or exactly 2 spans.
All inputs are finite; a program needn't handle non-finite values.
Results may differ from the reference program's by a relative error of at most 0.0064.
Values may be sent and summed in bfloat16 or wider, within the bound.
No kernel may reach another device: no remote copies, remote signals or barrier semaphores. Data moves between devices by JAX's collectives and lax.ppermute only.
A program may use at most 128 MiB of HBM per device.

```python
import math
import jax
import jax.numpy as jnp
from jax import lax

CHANNELS = 512
PANEL_DEV = 48
SAMPLES = 320
REPS = 4
PANELS = 3072
CAPACITY = 2
MIN_LEN = 214
FRAMES1 = 31
N_DP = 64


def draw_target(key, part):
    key = jax.random.fold_in(key, 1)

    def single(group_key):
        keys = jax.random.split(group_key, 4)
        order = jax.random.permutation(keys[0], N_DP)
        shifts = jax.random.permutation(keys[1], N_DP)[:PANEL_DEV // CAPACITY]
        ranks = jax.vmap(lambda k: jax.random.permutation(k, PANEL_DEV))(jax.random.split(keys[2], N_DP))
        slots = jax.vmap(lambda k: jax.random.permutation(k, PANEL_DEV))(jax.random.split(keys[3], N_DP))
        label = jnp.arange(N_DP)[:, None]
        dest_label = (label + shifts[ranks // CAPACITY]) % N_DP
        dest_slot = slots[dest_label, ranks]
        values = order[dest_label] * PANEL_DEV + dest_slot
        source = (order[:, None] * PANEL_DEV + jnp.arange(PANEL_DEV)[None, :]).reshape(-1)
        return jnp.zeros((N_DP * PANEL_DEV,), jnp.int32).at[source].set(values.reshape(-1).astype(jnp.int32))
    return jax.vmap(single)(jax.random.split(key, REPS))


def draw_lengths(key, part):
    key = jax.random.fold_in(key, 2)
    first, second = jax.random.split(key)
    values = jax.random.randint(first, (REPS, PANELS), MIN_LEN, SAMPLES + 1).astype(jnp.int32)
    chosen = jax.random.randint(second, (REPS,), 0, PANELS)
    return values.at[jnp.arange(REPS), chosen].set(SAMPLES)


def steps_of(key, dims, cuts, least, largest):
    factor_of = 1.0
    for dim, blocks in cuts:
        draws = jax.random.uniform(jax.random.fold_in(jax.random.fold_in(key, 6), dim), (blocks,), jnp.float32, least / len(cuts), largest / len(cuts))
        factor_of = factor_of * jnp.repeat(jnp.exp(draws), dims[dim] // blocks).reshape((-1,) + (1,) * (len(dims) - 1 - dim))
    return factor_of


def bell_draw(key, dims, width, bound, cuts=(), kind=jnp.bfloat16):
    array = jax.random.normal(key, dims, jnp.float32) * width
    if len(cuts) > 0:
        array = steps_of(key, dims, cuts, -0.22, 0.18) * array
    return jnp.clip(array, min=-bound, max=bound).astype(kind)


def setup_inputs(seed: int = 0) -> dict:
    streams_of = jax.random.split(jax.random.key(seed), 9)
    waveform = bell_draw(streams_of[0], (REPS, PANELS, SAMPLES), 1.0, 6.0, ((0, 4), (1, 64)))
    lengths = draw_lengths(jax.random.fold_in(streams_of[8], 71), 0)
    target = draw_target(jax.random.fold_in(streams_of[8], 71), 0)
    conv0_weight = bell_draw(streams_of[3], (10, CHANNELS), 10 ** -0.5, 2.0)
    norm_gain = jnp.clip(jax.random.uniform(streams_of[4], (CHANNELS,), jnp.float32, 0.5, 1.5), 0.5, 1.5)
    norm_bias = jnp.clip(jax.random.uniform(streams_of[5], (CHANNELS,), jnp.float32, -0.5, 0.5), -0.5, 0.5)
    conv1_weight = bell_draw(streams_of[6], (3, CHANNELS, CHANNELS), (3 * CHANNELS) ** -0.5, 0.15625)
    feature_grad = bell_draw(streams_of[7], (REPS, PANELS, FRAMES1, CHANNELS), 1.0, 6.0, ((0, 4), (1, 64)))
    return dict(waveform=waveform, lengths=lengths, target=target, conv0_weight=conv0_weight, norm_gain=norm_gain, norm_bias=norm_bias, conv1_weight=conv1_weight, feature_grad=feature_grad)


def product(form, left, right):
    return jnp.einsum(form, left.astype(jnp.float32), right.astype(jnp.float32), precision=lax.Precision.HIGHEST)

def gelu_and_slope(values):
    cumul = 0.5 * (1.0 + lax.erf(values * 0.7071067811865476))
    density = jnp.exp(-0.5 * values * values) * 0.3989422804014327
    return (values * cumul, cumul + values * density)

def encode(panels, panel_len, conv0_weight, norm_gain, norm_bias, conv1_weight, feature_grad, scale):
    panel_num, sample_num = panels.shape
    chans = conv0_weight.shape[1]
    frames_zero = (sample_num - 10) // 5 + 1
    frames_one = (frames_zero - 3) // 2 + 1
    pieces = panels[:, :5 * (frames_zero + 1)].reshape(panel_num, frames_zero + 1, 5)
    patches = jnp.concatenate([pieces[:, :-1], pieces[:, 1:]], axis=2)
    first_pre = product('ptk,kc->ptc', patches, conv0_weight)
    valid_zero = (panel_len - 10) // 5 + 1
    mask_zero = (jnp.arange(frames_zero)[None, :] < valid_zero[:, None]).astype(jnp.float32)[:, :, None]
    inverse = (1.0 / valid_zero.astype(jnp.float32))[:, None, None]
    center = lax.optimization_barrier(jnp.sum(first_pre * mask_zero, axis=1, keepdims=True)) * inverse
    centred = (first_pre - center) * mask_zero
    variance = lax.optimization_barrier(jnp.sum(centred * centred, axis=1, keepdims=True)) * inverse
    inv_std = lax.rsqrt(variance + 1e-05)
    normed = centred * inv_std
    act_zero, slope_zero = gelu_and_slope(normed * norm_gain + norm_bias)
    hidden = (act_zero * mask_zero).astype(jnp.bfloat16)
    taps = [hidden[:, k:k + 2 * frames_one - 1:2] for k in range(3)]
    second_pre = product('ptc,cd->ptd', taps[0], conv1_weight[0])
    second_pre = second_pre + product('ptc,cd->ptd', taps[1], conv1_weight[1])
    second_pre = second_pre + product('ptc,cd->ptd', taps[2], conv1_weight[2])
    valid_one = (valid_zero - 3) // 2 + 1
    mask_one = (jnp.arange(frames_one)[None, :] < valid_one[:, None]).astype(jnp.float32)[:, :, None]
    act_one, slope_one = gelu_and_slope(second_pre)
    features = (act_one * mask_one).astype(jnp.bfloat16)
    grad_one = (feature_grad.astype(jnp.float32) * scale * mask_one * slope_one).astype(jnp.bfloat16)
    weight_one = jnp.stack([product('ptc,ptd->cd', taps[k], grad_one) for k in range(3)])
    backs = [product('ptd,cd->ptc', grad_one, conv1_weight[k]) for k in range(3)]
    even_part = jnp.pad(backs[0], ((0, 0), (0, 1), (0, 0))) + jnp.pad(backs[2], ((0, 0), (1, 0), (0, 0)))
    odd_part = jnp.pad(backs[1], ((0, 0), (0, 1), (0, 0)))
    dhidden = jnp.stack([even_part, odd_part], axis=2).reshape(panel_num, 2 * frames_one + 2, chans)[:, :frames_zero]
    dpre = dhidden * mask_zero * slope_zero
    grad_b = lax.optimization_barrier(jnp.sum(dpre, axis=(0, 1)))
    grad_g = lax.optimization_barrier(jnp.sum(dpre * normed, axis=(0, 1)))
    dnorm = dpre * norm_gain
    mean_d = lax.optimization_barrier(jnp.sum(dnorm, axis=1, keepdims=True)) * inverse
    mean_dn = lax.optimization_barrier(jnp.sum(dnorm * normed, axis=1, keepdims=True)) * inverse
    dinput = (inv_std * (dnorm - mean_d - normed * mean_dn) * mask_zero).astype(jnp.bfloat16)
    weight_zero = product('ptk,ptc->kc', patches, dinput)
    rows = jnp.concatenate([weight_zero, grad_g[None], grad_b[None], weight_one.reshape(3 * chans, chans)], axis=0)
    return (features, rows)

def reference(waveform, lengths, target, conv0_weight, norm_gain, norm_bias, conv1_weight, feature_grad):
    moved = jax.vmap(lambda wave, dest: jnp.zeros_like(wave).at[dest].set(wave))(waveform, target)
    moved_len = jax.vmap(lambda lens, dest: jnp.zeros_like(lens).at[dest].set(lens))(lengths, target)
    scale = 1.0 / math.sqrt(REPS * PANELS * FRAMES1)
    blocks = REPS * N_DP
    wave_blocks = moved.reshape(blocks, PANEL_DEV, SAMPLES)
    len_blocks = moved_len.reshape(blocks, PANEL_DEV)
    grad_blocks = feature_grad.reshape(blocks, PANEL_DEV, FRAMES1, CHANNELS)

    def step(carry, item):
        feats, rows = encode(item[0], item[1], conv0_weight, norm_gain, norm_bias, conv1_weight, item[2], scale)
        return (carry + rows, feats)
    start = jnp.zeros((3 * CHANNELS + 12, CHANNELS), jnp.float32)
    total, feats = lax.scan(step, start, (wave_blocks, len_blocks, grad_blocks))
    features = feats.reshape(REPS, PANELS, FRAMES1, CHANNELS)
    return (features, total[:10], total[10], total[11], total[12:].reshape(3, CHANNELS, CHANNELS))
```

```python
import functools

import jax
import jax.numpy as jnp
import numpy as np
from jax import lax
from jax.experimental import pallas as pl
from jax.experimental.pallas import tpu as pltpu
from jax.sharding import PartitionSpec as P

BF, F32 = jnp.bfloat16, jnp.float32
VM = pl.BlockSpec(memory_space=pltpu.VMEM)
SM = pl.BlockSpec(memory_space=pltpu.SMEM)
BOTH = ("dp", "rep")
SAMPLES = 320


def call(kernel, outs, ins, scal=None, scratch=(), limit=48):
    specs = [VM] * len(ins)
    if scal is not None:
        specs = [SM] + specs
        ins = [scal] + list(ins)
    shapes = [jax.ShapeDtypeStruct(s, d) for s, d in outs]
    return pl.pallas_call(
        kernel,
        out_shape=shapes,
        in_specs=specs,
        out_specs=[VM] * len(outs),
        scratch_shapes=[pltpu.VMEM(s, d) for s, d in scratch],
        compiler_params=pltpu.CompilerParams(vmem_limit_bytes=limit << 20),
    )(*ins)


def perms():
    every = [(z, y, c, x) for z in range(8) for y in range(4) for c in range(2) for x in range(4)]

    def lin(z, y, c, x):
        return ((z * 4 + y) * 2 + c) * 4 + x

    def build(move):
        return [(lin(*p), lin(*move(*p))) for p in every]

    def along(first, k):
        def move(z, y, c, x):
            if (c == 0) == first:
                return (z, y, c, (x + k) % 4)
            return (z, (y + k) % 4, c, x)

        return build(move)

    core = build(lambda z, y, c, x: (z, y, 1 - c, x))
    one = [along(True, k) for k in range(1, 4)]
    two = [along(False, k) for k in range(1, 4)]
    pair = build(lambda z, y, c, x: (z ^ 1, y, c, x))
    quad = [build(lambda z, y, c, x, k=k: ((z + 2 * k) % 8, y, c, x)) for k in range(1, 4)]
    return core, one, two, pair, quad


def send(value, perm):
    return lax.ppermute(value, BOTH, perm)


def split(value):
    high = value.astype(BF)
    return high, (value - high.astype(F32)).astype(BF)


def k_scatter_one(pos, own, got, m1, m2, m3, keep):
    a1, core = pos[0], pos[2]
    for k, out in ((0, None), (1, m1), (2, m2), (3, m3)):
        j = (a1 + k) & 3
        mine = pl.ds(pl.multiple_of(core * 768 + j * 192, 192), 192)
        theirs = pl.ds(pl.multiple_of(j * 192, 192), 192)
        total = own[mine, :] + got[theirs, :].astype(F32)
        if out is None:
            keep[...] = total
        else:
            out[...] = total.astype(BF)


def k_scatter_two(pos, keep, r1, r2, r3, small_a, small_b, m1, m2, m3, keep2, small):
    a2 = pos[1]
    for k, out in ((0, None), (1, m1), (2, m2), (3, m3)):
        rows = pl.ds(pl.multiple_of(((a2 + k) & 3) * 48, 16), 48)
        total = keep[rows, :] + r1[rows, :].astype(F32) + r2[rows, :].astype(F32) + r3[rows, :].astype(F32)
        if out is None:
            keep2[...] = total
        else:
            out[pl.ds(0, 48), :] = total.astype(BF)
    high, low = split(small_a[...] + small_b[...])
    small[pl.ds(0, 16), :] = high
    small[pl.ds(16, 16), :] = low
    for out in (m1, m2, m3):
        out[pl.ds(48, 16), :] = high
        out[pl.ds(64, 16), :] = low


def lift(ref, at):
    return ref[pl.ds(at, 16), :].astype(F32) + ref[pl.ds(at + 16, 16), :].astype(F32)


def put(out, at, value):
    high, low = split(value)
    out[pl.ds(at, 16), :] = high
    out[pl.ds(at + 16, 16), :] = low


def k_sum_two(keep2, small, r1, r2, r3, out):
    head = pl.ds(0, 48)
    out[head, :] = (
        (keep2[...] + r2[head, :].astype(F32)) + (r1[head, :].astype(F32) + r3[head, :].astype(F32))
    ).astype(BF)
    put(out, 48, (lift(small, 0) + lift(r2, 48)) + (lift(r1, 48) + lift(r3, 48)))


def k_pair(a, b, out):
    head = pl.ds(0, 48)
    out[head, :] = (a[head, :].astype(F32) + b[head, :].astype(F32)).astype(BF)
    put(out, 48, lift(a, 48) + lift(b, 48))


def k_quad(a, r1, r2, r3, out, small):
    head = pl.ds(0, 48)
    out[...] = (
        (a[head, :].astype(F32) + r2[head, :].astype(F32)) + (r1[head, :].astype(F32) + r3[head, :].astype(F32))
    ).astype(BF)
    put(small, 0, (lift(a, 48) + lift(r2, 48)) + (lift(r1, 48) + lift(r3, 48)))


def k_join_two(own, r1, r2, r3, small, out):
    for k, part in enumerate((own, r1, r2, r3)):
        out[pl.ds(48 * k, 48), :] = part[...]
    out[pl.ds(192, 32), :] = small[...]


def k_join_one(own, r1, r2, r3, out):
    for k, part in enumerate((own, r1, r2, r3)):
        out[pl.ds(192 * k, 192), :] = part[pl.ds(0, 192), :]
    put(out, 768, (lift(own, 192) + lift(r2, 192)) + (lift(r1, 192) + lift(r3, 192)))


def k_final(pos, own, got, out, small):
    small[...] = 0.5 * (lift(own, 768) + lift(got, 768))
    core, x, y = pos[2], pos[3], pos[4]

    def place(ref, base, first, second):
        for j1 in range(4):
            for j2 in range(4):
                at = ((first - j1) & 3) * 4 + ((second - j2) & 3)
                out[pl.ds(base + (j1 * 4 + j2) * 48, 48), :] = ref[pl.ds(pl.multiple_of(at * 48, 16), 48), :].astype(F32)

    @pl.when(core == 0)
    def _():
        place(own, 0, x, y)
        place(got, 768, y, x)

    @pl.when(core == 1)
    def _():
        place(got, 0, x, y)
        place(own, 768, y, x)


def where_am_i():
    dp, x = lax.axis_index("dp"), lax.axis_index("rep")
    core, y = dp % 2, (dp // 2) % 4
    first = jnp.where(core == 0, x, y)
    second = jnp.where(core == 0, y, x)
    return jnp.stack([first, second, core, x, y]).astype(jnp.int32)


def reduce_all(pos, own, other, small):
    core, one, two, pair, quad = perms()
    row = 512
    got = send(other, core)
    m1, m2, m3, keep = call(
        k_scatter_one, [((192, row), BF)] * 3 + [((192, row), F32)], [own, got], pos
    )
    small_b = send(small, core)
    r = [send(m, p) for m, p in zip((m1, m2, m3), one)]
    m1, m2, m3, keep2, s = call(
        k_scatter_two,
        [((80, row), BF)] * 3 + [((48, row), F32), ((32, row), BF)],
        [keep, *r, small, small_b],
        pos,
    )
    r = [send(m, p) for m, p in zip((m1, m2, m3), two)]
    (a,) = call(k_sum_two, [((80, row), BF)], [keep2, s, *r])
    b = send(a, pair)
    (a,) = call(k_pair, [((80, row), BF)], [a, b])
    r = [send(a, p) for p in quad]
    a, s = call(k_quad, [((48, row), BF), ((32, row), BF)], [a, *r])
    r = [send(a, p) for p in two]
    (a,) = call(k_join_two, [((224, row), BF)], [a, *r, s])
    r = [send(a, p) for p in one]
    (a,) = call(k_join_one, [((800, row), BF)], [a, *r])
    got = send(a, core)
    return call(k_final, [((1536, row), F32), ((16, row), F32)], [a, got], pos)


WIDE = 384


def k_pack(wave, length, target, out, rows):
    spans = wave.shape[0]
    goal = target[...].astype(F32)
    device = jnp.floor((goal + 0.5) * (1.0 / spans))
    slot = goal - device * spans
    up = lax.broadcasted_iota(jnp.int32, (spans, spans), 0)
    across = lax.broadcasted_iota(jnp.int32, (spans, spans), 1)

    def column(row):
        return jnp.sum(jnp.where(up == across, jnp.broadcast_to(row, (spans, spans)), 0.0), axis=1, keepdims=True)

    same = (column(device) == device) & (up < across)
    rank = jnp.sum(jnp.where(same, 1.0, 0.0), axis=0, keepdims=True)
    bucket = (device * 2.0 + rank).astype(jnp.int32)
    places = out.shape[0]
    pick = lax.broadcasted_iota(jnp.int32, (places, spans), 0) == bucket
    pick = jnp.where(pick, 1.0, 0.0).astype(BF)
    rows[...] = jnp.zeros(rows.shape, F32)
    rows[:, pl.ds(0, SAMPLES)] = wave[...].astype(F32)
    lane = lax.broadcasted_iota(jnp.int32, (spans, 128), 1)
    tail = rows[:, pl.ds(256, 128)]
    tail = jnp.where(lane == SAMPLES - 256, column(slot) + 1.0, tail)
    tail = jnp.where(lane == SAMPLES - 255, column(length[...].astype(F32)) - 214.0, tail)
    rows[:, pl.ds(256, 128)] = tail
    out[...] = jnp.dot(pick, rows[...].astype(BF), preferred_element_type=F32).astype(BF)


def gelu_parts(value):
    cumul = 0.5 * (1.0 + lax.erf(value * 0.7071067811865476))
    density = jnp.exp(-0.5 * value * value) * 0.3989422804014327
    return cumul, density


BLOCK = 8
ROWS = 32 * BLOCK


def tall(rows):
    return jnp.concatenate([rows] * 4, axis=0)


def dot_t(left, right):
    return lax.dot_general(left, right, (((0,), (0,)), ((), ())), preferred_element_type=F32)


def dot_nt(left, right):
    return lax.dot_general(left, right, (((1,), (1,)), ((), ())), preferred_element_type=F32)


def k_forward(
    scale, pos, arrived, fold, weo, gain, bias, weight, fgrad,
    feats, g, gs, se, so, ne, no, istd, valid, x, full, other,
    panels, window, am, pre, he, ho, hs, pre1,
):
    spans = panels.shape[0]
    arr = arrived[...]
    lane = lax.broadcasted_iota(jnp.int32, (128, 128), 1).astype(F32)
    meta = arr[:, 256:384].astype(F32)
    slot = meta[:, SAMPLES - 256 : SAMPLES - 255]
    place = jnp.where(slot - 1.0 == lane, 1.0, 0.0).astype(BF)
    moved = dot_t(place, arr)[0:spans]
    panels[...] = jnp.broadcast_to(moved[:, None, :], panels.shape)
    length = moved[:, SAMPLES + 1 : SAMPLES + 2] + 214.0
    count = jnp.broadcast_to(jnp.floor((length - 9.5) * 0.2) + 1.0, (spans, 128))
    valid[...] = jnp.broadcast_to(count[:, None, :], valid.shape)
    step = lax.broadcasted_iota(jnp.int32, (32, WIDE), 0) * 10
    sample = lax.broadcasted_iota(jnp.int32, (32, WIDE), 1)
    window[:, pl.ds(0, WIDE)] = jnp.where((sample >= step) & (sample < step + 10), 1.0, 0.0)
    window[:, pl.ds(WIDE, WIDE)] = jnp.where((sample >= step + 5) & (sample < step + 15), 1.0, 0.0)
    frame = lax.broadcasted_iota(jnp.int32, (32, 128), 0).astype(F32)

    def block(b, carry):
        base = b * BLOCK

        def patch(q, carry):
            p = base + q
            count = tall(valid[p])
            keep_e, keep_o = 2.0 * frame < count, 2.0 * frame + 1.0 < count
            rows = pl.ds(pl.multiple_of(q * 32, 32), 32)
            for t in range(6):
                part = tall(panels[p, :, pl.ds((t % 3) * 128, 128)])
                part = jnp.where(keep_e if t < 3 else keep_o, part * window[:, pl.ds(t * 128, 128)], 0.0)
                am[rows, pl.ds(t * 128, 128)] = part.astype(BF)
            return carry

        lax.fori_loop(0, BLOCK, patch, 0)
        every = pl.ds(pl.multiple_of(b * ROWS, ROWS), ROWS)
        xs = jnp.dot(am[...], fold[...], preferred_element_type=F32).astype(BF)
        x[every, :] = xs
        pre[...] = jnp.dot(xs, weo[...], preferred_element_type=F32)

        def norm(q, carry):
            p = base + q
            count = valid[p]
            inverse = 1.0 / count[0:1]
            wide = tall(count)
            keep_e, keep_o = 2.0 * frame < wide, 2.0 * frame + 1.0 < wide
            rows = pl.ds(pl.multiple_of(q * 32, 32), 32)
            at = pl.ds(pl.multiple_of(p * 32, 32), 32)
            for t in range(4):
                cols = pl.ds(t * 128, 128)
                e = pre[rows, cols]
                o = pre[rows, pl.ds(512 + t * 128, 128)]
                center = jnp.sum(e + o, axis=0, keepdims=True) * inverse
                e = jnp.where(keep_e, e - center, 0.0)
                o = jnp.where(keep_o, o - center, 0.0)
                variance = jnp.sum(e * e + o * o, axis=0, keepdims=True) * inverse
                rs = lax.rsqrt(variance + 1e-05)
                istd[p, :, cols] = jnp.broadcast_to(rs, (8, 128))
                scale_row, bias_row = gain[:, cols], bias[:, cols]
                for value, keep, n_ref, s_ref, h_ref in ((e, keep_e, ne, se, he), (o, keep_o, no, so, ho)):
                    value = value * rs
                    n_ref[at, cols] = value.astype(BF)
                    value = value * scale_row + bias_row
                    cumul, density = gelu_parts(value)
                    hidden = jnp.where(keep, value * cumul, 0.0)
                    s_ref[at, cols] = jnp.where(keep, cumul + value * density, 0.0).astype(BF)
                    h_ref[at, cols] = hidden.astype(BF)
                    if h_ref is he:
                        hs[rows, cols] = pltpu.roll(hidden, 31, 0).astype(BF)
            return carry

        lax.fori_loop(0, BLOCK, norm, 0)
        pre1[...] = (
            jnp.dot(he[every, :], weight[0], preferred_element_type=F32)
            + jnp.dot(ho[every, :], weight[1], preferred_element_type=F32)
            + jnp.dot(hs[...], weight[2], preferred_element_type=F32)
        )

        def second(q, carry):
            p = base + q
            count = tall(jnp.floor((valid[p] - 2.5) * 0.5) + 1.0)
            keep = frame < count
            rows = pl.ds(pl.multiple_of(q * 32, 32), 32)
            at = pl.ds(pl.multiple_of(p * 32, 32), 32)
            for t in range(4):
                cols = pl.ds(t * 128, 128)
                value = pre1[rows, cols]
                cumul, density = gelu_parts(value)
                act = jnp.where(keep, value * cumul, 0.0)
                feats[p, :, cols] = act[0:31].astype(BF)
                up = fgrad[p, :, cols].astype(F32) * scale
                up = jnp.concatenate([up, jnp.zeros((1, 128), F32)], axis=0)
                grad = jnp.where(keep, up * (cumul + value * density), 0.0)
                g[at, cols] = grad.astype(BF)
                gs[at, cols] = pltpu.roll(grad, 1, 0).astype(BF)
            return carry

        lax.fori_loop(0, BLOCK, second, 0)
        return carry

    lax.fori_loop(0, spans // BLOCK, block, 0)
    full[pl.ds(0, 512), :] = dot_t(he[...], g[...])
    full[pl.ds(512, 512), :] = dot_t(ho[...], g[...])
    full[pl.ds(1024, 512), :] = dot_t(he[...], gs[...])
    away = pl.ds(pl.multiple_of((1 - pos[2]) * 768, 768), 768)
    other[...] = full[away, :].astype(BF)


def k_backward(
    g, gs, se, so, ne, no, istd, valid, x, gain, weight, small,
    de, do, dxe, dxo, sums,
):
    spans = istd.shape[0]
    sums[...] = jnp.zeros(sums.shape, F32)

    def block(b, carry):
        base = b * BLOCK
        every = pl.ds(pl.multiple_of(b * ROWS, ROWS), ROWS)
        de[...] = dot_nt(g[every, :], weight[0]) + dot_nt(gs[every, :], weight[2])
        do[...] = dot_nt(g[every, :], weight[1])

        def back(q, carry):
            p = base + q
            inverse = 1.0 / valid[p, pl.ds(0, 1), :]
            rows = pl.ds(pl.multiple_of(q * 32, 32), 32)
            at = pl.ds(pl.multiple_of(p * 32, 32), 32)
            for t in range(4):
                cols = pl.ds(t * 128, 128)
                pe = de[rows, cols] * se[at, cols].astype(F32)
                po = do[rows, cols] * so[at, cols].astype(F32)
                e, o = ne[at, cols].astype(F32), no[at, cols].astype(F32)
                plain = jnp.sum(pe + po, axis=0, keepdims=True)
                mixed = jnp.sum(pe * e + po * o, axis=0, keepdims=True)
                sums[pl.ds(0, 1), cols] += mixed
                sums[pl.ds(1, 1), cols] += plain
                lead = istd[p, pl.ds(0, 1), cols] * gain[:, cols]
                plain, mixed = plain * inverse, mixed * inverse
                dxe[at, cols] = ((pe - plain - e * mixed) * lead).astype(BF)
                dxo[at, cols] = ((po - plain - o * mixed) * lead).astype(BF)
            return carry

        lax.fori_loop(0, BLOCK, back, 0)
        return carry

    lax.fori_loop(0, spans // BLOCK, block, 0)
    small[...] = dot_t(x[...], dxe[...])[0:16] + dot_t(x[...], dxo[...])[16:32]
    small[pl.ds(10, 1), :] = sums[pl.ds(0, 1), :]
    small[pl.ds(11, 1), :] = sums[pl.ds(1, 1), :]


def folding():
    table = np.zeros((2 * WIDE, 128), np.float32)
    for s in range(SAMPLES):
        table[s, s % 10] = 1.0
        if s >= 5:
            table[WIDE + s, 16 + (s - 5) % 10] = 1.0
    return jnp.asarray(table, BF)


def encode(pos, arrived, conv0_weight, norm_gain, norm_bias, conv1_weight, feature_grad, scale):
    spans = feature_grad.shape[0]
    rows = spans * 32
    zero = jnp.zeros
    weo = jnp.concatenate(
        [
            jnp.concatenate([conv0_weight, zero((6, 512), BF), zero((16, 512), BF)], axis=0),
            jnp.concatenate([zero((16, 512), BF), conv0_weight, zero((6, 512), BF)], axis=0),
        ],
        axis=1,
    )
    weo = jnp.concatenate([weo, zero((96, 1024), BF)], axis=0)
    gain, bias = norm_gain[None], norm_bias[None]
    wide = ((rows, 512), BF)
    feats, g, gs, se, so, ne, no, istd, valid, x, full, other = call(
        functools.partial(k_forward, scale),
        [
            (feature_grad.shape, BF), wide, wide, wide, wide, wide, wide,
            ((spans, 8, 512), F32), ((spans, 8, 128), F32), ((rows, 128), BF), ((1536, 512), F32), ((768, 512), BF),
        ],
        [arrived, folding(), weo, gain, bias, conv1_weight, feature_grad],
        pos,
        scratch=[
            ((spans, 8, WIDE), F32), ((32, 2 * WIDE), F32), ((ROWS, 2 * WIDE), BF), ((ROWS, 1024), F32),
            ((rows, 512), BF), ((rows, 512), BF), ((ROWS, 512), BF), ((ROWS, 512), F32),
        ],
    )
    (small,) = call(
        k_backward,
        [((16, 512), F32)],
        [g, gs, se, so, ne, no, istd, valid, x, gain, conv1_weight],
        scratch=[((ROWS, 512), F32), ((ROWS, 512), F32), ((rows, 512), BF), ((rows, 512), BF), ((8, 512), F32)],
    )
    return feats, full, other, small


def body(waveform, lengths, target, conv0_weight, norm_gain, norm_bias, conv1_weight, feature_grad):
    spans = waveform.shape[1]
    devices = lax.axis_size("dp")
    frames = feature_grad.shape[2]
    pos = where_am_i()
    (packed,) = call(
        k_pack, [((2 * devices, WIDE), BF)], [waveform[0], lengths, target], scratch=[((spans, WIDE), F32)]
    )
    arrived = lax.all_to_all(packed.reshape(devices, 2, WIDE), "dp", split_axis=0, concat_axis=0, tiled=True)
    arrived = arrived.reshape(2 * devices, WIDE)
    scale = 1.0 / float(lax.axis_size("rep") * devices * spans * frames) ** 0.5
    feats, full, other, small = encode(
        pos, arrived, conv0_weight, norm_gain, norm_bias, conv1_weight, feature_grad[0], scale
    )
    full, small = reduce_all(pos, full, other, small)
    return (feats[None], small[:10], small[10], small[11], full.reshape(conv1_weight.shape))


def solution(mesh):
    placed = (
        P("rep", "dp", None),
        P("rep", "dp"),
        P("rep", "dp"),
        P(),
        P(),
        P(),
        P(),
        P("rep", "dp", None, None),
    )
    return jax.shard_map(
        body,
        mesh=mesh,
        in_specs=placed,
        out_specs=(P("rep", "dp", None, None), P(), P(), P(), P()),
        check_vma=False,
    )
```

```python
import functools

import jax
import jax.numpy as jnp
import numpy as np
from jax import lax
from jax.experimental import pallas as pl
from jax.experimental.pallas import tpu as pltpu
from jax.sharding import PartitionSpec as P

BF, F32 = jnp.bfloat16, jnp.float32
VM = pl.BlockSpec(memory_space=pltpu.VMEM)
SM = pl.BlockSpec(memory_space=pltpu.SMEM)
ANY = pl.BlockSpec(memory_space=pl.ANY)
HBM = pl.BlockSpec(memory_space=pltpu.HBM)
BOTH = ("dp", "rep")
SAMPLES = 320


def call(kernel, outs, ins, scal=None, scratch=(), after=(), late=ANY, limit=20):
    specs = [VM] * len(ins) + [late] * len(after)
    ins = [*ins, *after]
    if scal is not None:
        specs = [SM] + specs
        ins = [scal, *ins]
    shapes = [jax.ShapeDtypeStruct(s, d) for s, d in outs]
    return pl.pallas_call(
        kernel,
        out_shape=shapes,
        in_specs=specs,
        out_specs=[VM] * len(outs),
        scratch_shapes=[pltpu.VMEM(*s) if isinstance(s, tuple) else s for s in scratch],
        compiler_params=pltpu.CompilerParams(vmem_limit_bytes=limit << 20),
    )(*ins)


def perms():
    every = [(z, y, c, x) for z in range(8) for y in range(4) for c in range(2) for x in range(4)]

    def lin(z, y, c, x):
        return ((z * 4 + y) * 2 + c) * 4 + x

    def build(move):
        return [(lin(*p), lin(*move(*p))) for p in every]

    def along(first, k):
        def move(z, y, c, x):
            if (c == 0) == first:
                return (z, y, c, (x + k) % 4)
            return (z, (y + k) % 4, c, x)

        return build(move)

    core = build(lambda z, y, c, x: (z, y, 1 - c, x))
    one = [along(True, k) for k in range(1, 4)]
    two = [along(False, k) for k in range(1, 4)]
    steps = [build(lambda z, y, c, x, flip=flip: (z ^ flip, y, c, x)) for flip in (1, 3, 7)]
    return core, one, two, steps


def send(value, perm):
    return lax.ppermute(value, BOTH, perm)


def k_scatter_one(pos, own, got, before, m1, m2, m3, keep):
    a1, core = pos[0], pos[2]
    for k, out in ((0, None), (1, m1), (2, m2), (3, m3)):
        j = (a1 + k) & 3
        mine = pl.ds(pl.multiple_of(core * 768 + j * 192, 192), 192)
        theirs = pl.ds(pl.multiple_of(j * 192, 192), 192)
        total = own[mine, :] + got[theirs, :].astype(F32)
        if out is None:
            keep[...] = total
        else:
            out[...] = total.astype(BF)


def k_scatter_two(pos, keep, r1, r2, r3, before, m1, m2, m3, keep2):
    a2 = pos[1]
    for k, out in ((0, None), (1, m1), (2, m2), (3, m3)):
        rows = pl.ds(pl.multiple_of(((a2 + k) & 3) * 48, 16), 48)
        total = keep[rows, :] + r1[rows, :].astype(F32) + r2[rows, :].astype(F32) + r3[rows, :].astype(F32)
        if out is None:
            keep2[...] = total
        else:
            out[...] = total.astype(BF)


def lift(ref, at):
    return ref[pl.ds(at, 16), :].astype(F32) + ref[pl.ds(at + 16, 16), :].astype(F32)


def put(out, at, value):
    high = value.astype(BF)
    out[pl.ds(at, 16), :] = high
    out[pl.ds(at + 16, 16), :] = (value - high.astype(F32)).astype(BF)


def k_sum_two(keep2, r1, r2, r3, small, out):
    out[pl.ds(0, 48), :] = (
        (keep2[...] + r2[...].astype(F32)) + (r1[...].astype(F32) + r3[...].astype(F32))
    ).astype(BF)
    put(out, 48, small[...])


def k_pair(a, b, out):
    head = pl.ds(0, 48)
    out[head, :] = (a[head, :].astype(F32) + b[head, :].astype(F32)).astype(BF)
    put(out, 48, lift(a, 48) + lift(b, 48))


def k_join_two(own, r1, r2, r3, out):
    for k, part in enumerate((own, r1, r2, r3)):
        out[pl.ds(48 * k, 48), :] = part[pl.ds(0, 48), :]
    put(out, 192, (lift(own, 48) + lift(r2, 48)) + (lift(r1, 48) + lift(r3, 48)))


def k_join_one(own, r1, r2, r3, out):
    for k, part in enumerate((own, r1, r2, r3)):
        out[pl.ds(192 * k, 192), :] = part[pl.ds(0, 192), :]
    put(out, 768, (lift(own, 192) + lift(r2, 192)) + (lift(r1, 192) + lift(r3, 192)))


def order(ref, out, j1, first, second):
    for j2 in range(4):
        at = ((first - j1) & 3) * 4 + ((second - j2) & 3)
        out[pl.ds((j1 * 4 + j2) * 48, 48), :] = ref[pl.ds(pl.multiple_of(at * 48, 16), 48), :].astype(F32)


def k_order(pos, own, out):
    for j1 in range(4):
        order(own, out, j1, pos[0], pos[1])


def k_final(pos, ready, own, got, full, conv0, gain, bias, rest, sems):
    core = pos[2]
    mine = pltpu.make_async_copy(ready, full.at[pl.ds(pl.multiple_of(core * 768, 768), 768), :], sems.at[0])
    mine.start()
    copies = []
    for j1 in range(4):
        order(got, rest, j1, pos[1], pos[0])
        at = pl.multiple_of((1 - core) * 768 + j1 * 192, 192)
        copy = pltpu.make_async_copy(rest.at[pl.ds(j1 * 192, 192), :], full.at[pl.ds(at, 192), :], sems.at[1 + j1])
        copy.start()
        copies.append(copy)
    total = lift(own, 768) + lift(got, 768)
    conv0[...] = total[0:10]
    gain[...] = total[10:11]
    bias[...] = total[11:12]
    mine.wait()
    for copy in copies:
        copy.wait()


def where_am_i():
    dp, x = lax.axis_index("dp"), lax.axis_index("rep")
    core, y = lax.rem(dp, 2), lax.rem(lax.div(dp, 2), 4)
    first = jnp.where(core == 0, x, y)
    second = jnp.where(core == 0, y, x)
    return jnp.stack([first, second, core]).astype(jnp.int32)


def reduce_all(pos, own, other, backward, feats):
    core, one, two, steps = perms()
    row = 512
    third = ((48, row), BF)
    got = send(other, core)
    small = backward(0, jnp.zeros((16, row), F32), other)
    m1, m2, m3, keep = call(
        k_scatter_one, [((192, row), BF)] * 3 + [((192, row), F32)], [own, got], pos, after=[small]
    )
    r = [send(m, p) for m, p in zip((m1, m2, m3), one)]
    small = backward(1, small, keep)
    m1, m2, m3, keep2 = call(
        k_scatter_two, [third] * 3 + [((48, row), F32)], [keep, *r], pos, after=[small]
    )
    r = [send(m, p) for m, p in zip((m1, m2, m3), two)]
    small = backward(2, small, keep2)
    (a,) = call(k_sum_two, [((80, row), BF)], [keep2, *r, small])
    for step in steps:
        b = send(a, step)
        (a,) = call(k_pair, [((80, row), BF)], [a, b])
    r = [send(a, p) for p in two]
    (a,) = call(k_join_two, [((224, row), BF)], [a, *r])
    feats = jnp.transpose(feats, (1, 0, 2))
    r = [send(a, p) for p in one]
    a, feats, *r = lax.optimization_barrier((a, feats, *r))
    (a,) = call(k_join_one, [((800, row), BF)], [a, *r])
    got = send(a, core)
    (ready,) = call(k_order, [((768, row), F32)], [a], pos)
    full, conv0, gain, bias = pl.pallas_call(
        k_final,
        out_shape=[jax.ShapeDtypeStruct((n, row), F32) for n in (1536, 10, 1, 1)],
        in_specs=[SM, VM, VM, VM],
        out_specs=[ANY, VM, VM, VM],
        scratch_shapes=[pltpu.VMEM((768, row), F32), pltpu.SemaphoreType.DMA((5,))],
        compiler_params=pltpu.CompilerParams(vmem_limit_bytes=20 << 20),
    )(pos, ready, a, got)
    return full, conv0, gain[0], bias[0], jnp.transpose(feats, (1, 0, 2))


WIDE = 384


def k_pack(wave_in, length_in, target_in, out, rows, wave, length, target, sems):
    copies = [
        pltpu.make_async_copy(source, place, sems.at[n])
        for n, (source, place) in enumerate(((wave_in, wave), (length_in, length), (target_in, target)))
    ]
    for copy in copies:
        copy.start()
    for copy in copies:
        copy.wait()
    spans = wave.shape[0]
    goal = target[...].astype(F32)
    device = jnp.floor((goal + 0.5) * (1.0 / spans))
    slot = goal - device * spans
    up = lax.broadcasted_iota(jnp.int32, (spans, spans), 0)
    across = lax.broadcasted_iota(jnp.int32, (spans, spans), 1)

    def column(row):
        return jnp.sum(jnp.where(up == across, jnp.broadcast_to(row, (spans, spans)), 0.0), axis=1, keepdims=True)

    same = (column(device) == device) & (up < across)
    rank = jnp.sum(jnp.where(same, 1.0, 0.0), axis=0, keepdims=True)
    bucket = (device * 2.0 + rank).astype(jnp.int32)
    places = out.shape[0]
    pick = lax.broadcasted_iota(jnp.int32, (places, spans), 0) == bucket
    pick = jnp.where(pick, 1.0, 0.0).astype(BF)
    rows[...] = jnp.zeros(rows.shape, F32)
    rows[:, pl.ds(0, SAMPLES)] = wave[...].astype(F32)
    lane = lax.broadcasted_iota(jnp.int32, (spans, 128), 1)
    tail = rows[:, pl.ds(256, 128)]
    tail = jnp.where(lane == SAMPLES - 256, column(slot) + 1.0, tail)
    tail = jnp.where(lane == SAMPLES - 255, column(length[...].astype(F32)) - 214.0, tail)
    rows[:, pl.ds(256, 128)] = tail
    out[...] = jnp.dot(pick, rows[...].astype(BF), preferred_element_type=F32).astype(BF)


def gelu_parts(value):
    cumul = 0.5 * (1.0 + lax.erf(value * 0.7071067811865476))
    density = jnp.exp(-0.5 * value * value) * 0.3989422804014327
    return cumul, density


BLOCK = 8
ROWS = 32 * BLOCK


def tall(rows):
    return jnp.concatenate([rows] * 4, axis=0)


def dot_t(left, right):
    return lax.dot_general(left, right, (((0,), (0,)), ((), ())), preferred_element_type=F32)


def dot_nt(left, right):
    return lax.dot_general(left, right, (((1,), (1,)), ((), ())), preferred_element_type=F32)


def k_forward(
    scale, pos, arrived, fold, weo, gain, bias, weight, fgrad,
    feats, g, gs, se, so, ne, no, istd, valid, x, full, other,
    panels, window, am, pre, he, ho, hs, pre1,
):
    spans = panels.shape[0]
    arr = arrived[...]
    lane = lax.broadcasted_iota(jnp.int32, (128, 128), 1).astype(F32)
    meta = arr[:, 256:384].astype(F32)
    slot = meta[:, SAMPLES - 256 : SAMPLES - 255]
    place = jnp.where(slot - 1.0 == lane, 1.0, 0.0).astype(BF)
    moved = dot_t(place, arr)[0:spans]
    panels[...] = jnp.broadcast_to(moved[:, None, :], panels.shape)
    length = moved[:, SAMPLES + 1 : SAMPLES + 2] + 214.0
    count = jnp.broadcast_to(jnp.floor((length - 9.5) * 0.2) + 1.0, (spans, 128))
    valid[...] = jnp.broadcast_to(count[:, None, :], valid.shape)
    step = lax.broadcasted_iota(jnp.int32, (32, WIDE), 0) * 10
    sample = lax.broadcasted_iota(jnp.int32, (32, WIDE), 1)
    window[:, pl.ds(0, WIDE)] = jnp.where((sample >= step) & (sample < step + 10), 1.0, 0.0)
    window[:, pl.ds(WIDE, WIDE)] = jnp.where((sample >= step + 5) & (sample < step + 15), 1.0, 0.0)
    frame = lax.broadcasted_iota(jnp.int32, (32, 128), 0).astype(F32)

    def block(b, carry):
        base = b * BLOCK

        def patch(q, carry):
            p = base + q
            count = tall(valid[p])
            keep_e, keep_o = 2.0 * frame < count, 2.0 * frame + 1.0 < count
            rows = pl.ds(pl.multiple_of(q * 32, 32), 32)
            for t in range(6):
                part = tall(panels[p, :, pl.ds((t % 3) * 128, 128)])
                part = jnp.where(keep_e if t < 3 else keep_o, part * window[:, pl.ds(t * 128, 128)], 0.0)
                am[rows, pl.ds(t * 128, 128)] = part.astype(BF)
            return carry

        lax.fori_loop(0, BLOCK, patch, 0, unroll=2)
        every = pl.ds(pl.multiple_of(b * ROWS, ROWS), ROWS)
        xs = jnp.dot(am[...], fold[...], preferred_element_type=F32).astype(BF)
        x[every, :] = xs
        pre[...] = jnp.dot(xs, weo[...], preferred_element_type=F32)

        def norm(q, carry):
            p = base + q
            count = valid[p]
            inverse = 1.0 / count[0:1]
            wide = tall(count)
            keep_e, keep_o = 2.0 * frame < wide, 2.0 * frame + 1.0 < wide
            rows = pl.ds(pl.multiple_of(q * 32, 32), 32)
            at = pl.ds(pl.multiple_of(p * 32, 32), 32)
            for t in range(4):
                cols = pl.ds(t * 128, 128)
                e = pre[rows, cols]
                o = pre[rows, pl.ds(512 + t * 128, 128)]
                center = jnp.sum(e + o, axis=0, keepdims=True) * inverse
                e = jnp.where(keep_e, e - center, 0.0)
                o = jnp.where(keep_o, o - center, 0.0)
                variance = jnp.sum(e * e + o * o, axis=0, keepdims=True) * inverse
                rs = lax.rsqrt(variance + 1e-05)
                istd[p, :, cols] = jnp.broadcast_to(rs, (8, 128))
                scale_row, bias_row = gain[:, cols], bias[:, cols]
                for value, keep, n_ref, s_ref, h_ref in ((e, keep_e, ne, se, he), (o, keep_o, no, so, ho)):
                    value = value * rs
                    n_ref[at, cols] = value.astype(BF)
                    value = value * scale_row + bias_row
                    cumul, density = gelu_parts(value)
                    hidden = jnp.where(keep, value * cumul, 0.0)
                    s_ref[at, cols] = jnp.where(keep, cumul + value * density, 0.0).astype(BF)
                    h_ref[at, cols] = hidden.astype(BF)
                    if h_ref is he:
                        hs[rows, cols] = pltpu.roll(hidden, 31, 0).astype(BF)
            return carry

        lax.fori_loop(0, BLOCK, norm, 0, unroll=2)
        pre1[...] = (
            jnp.dot(he[every, :], weight[0], preferred_element_type=F32)
            + jnp.dot(ho[every, :], weight[1], preferred_element_type=F32)
            + jnp.dot(hs[...], weight[2], preferred_element_type=F32)
        )

        def second(q, carry):
            p = base + q
            count = tall(jnp.floor((valid[p] - 2.5) * 0.5) + 1.0)
            keep = frame < count
            rows = pl.ds(pl.multiple_of(q * 32, 32), 32)
            at = pl.ds(pl.multiple_of(p * 32, 32), 32)
            for t in range(4):
                cols = pl.ds(t * 128, 128)
                value = pre1[rows, cols]
                cumul, density = gelu_parts(value)
                act = jnp.where(keep, value * cumul, 0.0)
                feats[p, :, cols] = act[0:31].astype(BF)
                up = fgrad[p, :, cols].astype(F32) * scale
                up = jnp.concatenate([up, jnp.zeros((1, 128), F32)], axis=0)
                grad = jnp.where(keep, up * (cumul + value * density), 0.0)
                g[at, cols] = grad.astype(BF)
                gs[at, cols] = pltpu.roll(grad, 1, 0).astype(BF)
            return carry

        lax.fori_loop(0, BLOCK, second, 0, unroll=2)
        return carry

    lax.fori_loop(0, spans // BLOCK, block, 0)
    full[pl.ds(0, 512), :] = dot_t(he[...], g[...])
    full[pl.ds(512, 512), :] = dot_t(ho[...], g[...])
    full[pl.ds(1024, 512), :] = dot_t(he[...], gs[...])
    away = pl.ds(pl.multiple_of((1 - pos[2]) * 768, 768), 768)
    other[...] = full[away, :].astype(BF)


def k_backward(
    step, g, gs, se, so, ne, no, istd, valid, x, gain, weight, start, before, small,
    de, do, dxe, dxo, sums,
):
    blocks = dxe.shape[0] // ROWS
    sums[...] = jnp.zeros(sums.shape, F32)

    def block(b, carry):
        base = (step * blocks + b) * BLOCK
        every = pl.ds(pl.multiple_of((step * blocks + b) * ROWS, ROWS), ROWS)
        de[...] = dot_nt(g[every, :], weight[0]) + dot_nt(gs[every, :], weight[2])
        do[...] = dot_nt(g[every, :], weight[1])

        def back(q, carry):
            p = base + q
            inverse = 1.0 / valid[p, pl.ds(0, 1), :]
            rows = pl.ds(pl.multiple_of(q * 32, 32), 32)
            at = pl.ds(pl.multiple_of(p * 32, 32), 32)
            here = pl.ds(pl.multiple_of((b * BLOCK + q) * 32, 32), 32)
            for t in range(4):
                cols = pl.ds(t * 128, 128)
                pe = de[rows, cols] * se[at, cols].astype(F32)
                po = do[rows, cols] * so[at, cols].astype(F32)
                e, o = ne[at, cols].astype(F32), no[at, cols].astype(F32)
                plain = jnp.sum(pe + po, axis=0, keepdims=True)
                mixed = jnp.sum(pe * e + po * o, axis=0, keepdims=True)
                sums[pl.ds(0, 1), cols] += mixed
                sums[pl.ds(1, 1), cols] += plain
                lead = istd[p, pl.ds(0, 1), cols] * gain[:, cols]
                plain, mixed = plain * inverse, mixed * inverse
                dxe[here, cols] = ((pe - plain - e * mixed) * lead).astype(BF)
                dxo[here, cols] = ((po - plain - o * mixed) * lead).astype(BF)
            return carry

        lax.fori_loop(0, BLOCK, back, 0, unroll=2)
        return carry

    lax.fori_loop(0, blocks, block, 0)
    part = x[pl.ds(step * blocks * ROWS, blocks * ROWS), :]
    small[...] = start[...] + dot_t(part, dxe[...])[0:16] + dot_t(part, dxo[...])[16:32]
    small[pl.ds(10, 2), :] += sums[pl.ds(0, 2), :]


def folding():
    table = np.zeros((2 * WIDE, 128), np.float32)
    for s in range(SAMPLES):
        table[s, s % 10] = 1.0
        if s >= 5:
            table[WIDE + s, 16 + (s - 5) % 10] = 1.0
    return jnp.asarray(table, BF)


def encode(pos, arrived, conv0_weight, norm_gain, norm_bias, conv1_weight, feature_grad, scale):
    spans = feature_grad.shape[0]
    rows = spans * 32
    zero = jnp.zeros
    weo = jnp.concatenate(
        [
            jnp.concatenate([conv0_weight, zero((6, 512), BF), zero((16, 512), BF)], axis=0),
            jnp.concatenate([zero((16, 512), BF), conv0_weight, zero((6, 512), BF)], axis=0),
        ],
        axis=1,
    )
    weo = jnp.concatenate([weo, zero((96, 1024), BF)], axis=0)
    gain, bias = norm_gain[None], norm_bias[None]
    wide = ((rows, 512), BF)
    feats, g, gs, se, so, ne, no, istd, valid, x, full, other = call(
        functools.partial(k_forward, scale),
        [
            (feature_grad.shape, BF), wide, wide, wide, wide, wide, wide,
            ((spans, 8, 512), F32), ((spans, 8, 128), F32), ((rows, 128), BF), ((1536, 512), F32), ((768, 512), BF),
        ],
        [arrived, folding(), weo, gain, bias, conv1_weight, feature_grad],
        pos,
        scratch=[
            ((spans, 8, WIDE), F32), ((32, 2 * WIDE), F32), ((ROWS, 2 * WIDE), BF), ((ROWS, 1024), F32),
            ((rows, 512), BF), ((rows, 512), BF), ((ROWS, 512), BF), ((ROWS, 512), F32),
        ],
    )

    def backward(step, small, before):
        part = (rows // 3, 512)
        return call(
            functools.partial(k_backward, step),
            [((16, 512), F32)],
            [g, gs, se, so, ne, no, istd, valid, x, gain, conv1_weight, small],
            scratch=[((ROWS, 512), F32), ((ROWS, 512), F32), (part, BF), (part, BF), ((8, 512), F32)],
            after=[before],
        )[0]

    return feats, full, other, backward


def body(waveform, lengths, target, conv0_weight, norm_gain, norm_bias, conv1_weight, feature_grad):
    spans = waveform.shape[1]
    devices = lax.axis_size("dp")
    frames = feature_grad.shape[2]
    pos = where_am_i()
    (packed,) = call(
        k_pack,
        [((2 * devices, WIDE), BF)],
        [],
        scratch=[
            ((spans, WIDE), F32), (waveform.shape[1:], BF), (lengths.shape, jnp.int32), (target.shape, jnp.int32),
            pltpu.SemaphoreType.DMA((3,)),
        ],
        after=[waveform[0], lengths, target],
        late=HBM,
    )
    arrived = lax.all_to_all(packed.reshape(devices, 2, WIDE), "dp", split_axis=0, concat_axis=0, tiled=True)
    arrived = arrived.reshape(2 * devices, WIDE)
    scale = 1.0 / float(lax.axis_size("rep") * devices * spans * frames) ** 0.5
    feats, full, other, backward = encode(
        pos, arrived, conv0_weight, norm_gain, norm_bias, conv1_weight, feature_grad[0], scale
    )
    full, conv0, gain, bias, feats = reduce_all(pos, full, other, backward, feats)
    return (feats[None], conv0, gain, bias, full.reshape(conv1_weight.shape))


def solution(mesh):
    placed = (
        P("rep", "dp", None),
        P("rep", "dp"),
        P("rep", "dp"),
        P(),
        P(),
        P(),
        P(),
        P("rep", "dp", None, None),
    )
    return jax.shard_map(
        body,
        mesh=mesh,
        in_specs=placed,
        out_specs=(P("rep", "dp", None, None), P(), P(), P(), P()),
        check_vma=False,
    )
```

```python
import functools

import jax
import jax.numpy as jnp
from jax import lax
from jax.experimental import pallas as pl
from jax.experimental.pallas import tpu as pltpu
from jax.sharding import PartitionSpec as P

BF, F32 = jnp.bfloat16, jnp.float32
VM = pl.BlockSpec(memory_space=pltpu.VMEM)
SM = pl.BlockSpec(memory_space=pltpu.SMEM)
ANY = pl.BlockSpec(memory_space=pl.ANY)
HBM = pl.BlockSpec(memory_space=pltpu.HBM)
BOTH = ("dp", "rep")
SAMPLES = 320


def call(kernel, outs, ins, scal=None, scratch=(), after=(), late=ANY, limit=20):
    specs = [VM] * len(ins) + [late] * len(after)
    ins = [*ins, *after]
    if scal is not None:
        specs = [SM] + specs
        ins = [scal, *ins]
    shapes = [jax.ShapeDtypeStruct(s, d) for s, d in outs]
    return pl.pallas_call(
        kernel,
        out_shape=shapes,
        in_specs=specs,
        out_specs=[VM] * len(outs),
        scratch_shapes=[pltpu.VMEM(*s) if isinstance(s, tuple) else s for s in scratch],
        compiler_params=pltpu.CompilerParams(vmem_limit_bytes=limit << 20),
    )(*ins)


def perms():
    every = [(z, y, c, x) for z in range(8) for y in range(4) for c in range(2) for x in range(4)]

    def lin(z, y, c, x):
        return ((z * 4 + y) * 2 + c) * 4 + x

    def build(move):
        return [(lin(*p), lin(*move(*p))) for p in every]

    def along(first, k):
        def move(z, y, c, x):
            if (c == 0) == first:
                return (z, y, c, (x + k) % 4)
            return (z, (y + k) % 4, c, x)

        return build(move)

    core = build(lambda z, y, c, x: (z, y, 1 - c, x))
    one = [along(True, k) for k in range(1, 4)]
    two = [along(False, k) for k in range(1, 4)]
    steps = [build(lambda z, y, c, x, flip=flip: (z ^ flip, y, c, x)) for flip in (1, 3, 7)]
    return core, one, two, steps


def send(value, perm):
    return lax.ppermute(value, BOTH, perm)


def k_scatter_one(pos, own, got, m1, m2, m3, keep):
    a1 = pos[0]
    for k, out in ((0, None), (1, m1), (2, m2), (3, m3)):
        j = (a1 + k) & 3
        rows = pl.ds(pl.multiple_of(j * 192, 192), 192)
        total = own[rows, :] + got[rows, :].astype(F32)
        if out is None:
            keep[...] = total
        else:
            out[...] = total.astype(BF)


def k_scatter_two(pos, keep, r1, r2, r3, before, m1, m2, m3, keep2):
    a2 = pos[1]
    for k, out in ((0, None), (1, m1), (2, m2), (3, m3)):
        rows = pl.ds(pl.multiple_of(((a2 + k) & 3) * 48, 16), 48)
        total = keep[rows, :] + r1[rows, :].astype(F32) + r2[rows, :].astype(F32) + r3[rows, :].astype(F32)
        if out is None:
            keep2[...] = total
        else:
            out[...] = total.astype(BF)


def lift(ref, at):
    return ref[pl.ds(at, 16), :].astype(F32) + ref[pl.ds(at + 16, 16), :].astype(F32)


def put(out, at, value):
    high = value.astype(BF)
    out[pl.ds(at, 16), :] = high
    out[pl.ds(at + 16, 16), :] = (value - high.astype(F32)).astype(BF)


def k_sum_two(keep2, r1, r2, r3, small, out):
    out[pl.ds(0, 48), :] = (
        (keep2[...] + r2[...].astype(F32)) + (r1[...].astype(F32) + r3[...].astype(F32))
    ).astype(BF)
    put(out, 48, small[...])


def k_pair(a, b, out):
    head = pl.ds(0, 48)
    out[head, :] = (a[head, :].astype(F32) + b[head, :].astype(F32)).astype(BF)
    put(out, 48, lift(a, 48) + lift(b, 48))


def k_join_two(own, r1, r2, r3, out):
    for k, part in enumerate((own, r1, r2, r3)):
        out[pl.ds(48 * k, 48), :] = part[pl.ds(0, 48), :]
    put(out, 192, (lift(own, 48) + lift(r2, 48)) + (lift(r1, 48) + lift(r3, 48)))


def k_join_one(own, r1, r2, r3, out):
    for k, part in enumerate((own, r1, r2, r3)):
        out[pl.ds(192 * k, 192), :] = part[pl.ds(0, 192), :]
    put(out, 768, (lift(own, 192) + lift(r2, 192)) + (lift(r1, 192) + lift(r3, 192)))


def order(ref, out, j1, first, second):
    for j2 in range(4):
        at = ((first - j1) & 3) * 4 + ((second - j2) & 3)
        out[pl.ds((j1 * 4 + j2) * 48, 48), :] = ref[pl.ds(pl.multiple_of(at * 48, 16), 48), :].astype(F32)


def flush(core, out, rest, sems, ref, first, second):
    copies = []
    for j1 in range(4):
        order(ref, rest, j1, first, second)
        at = pl.multiple_of(core * 768 + j1 * 192, 192)
        copy = pltpu.make_async_copy(rest.at[pl.ds(j1 * 192, 192), :], out.at[pl.ds(at, 192), :], sems.at[j1])
        copy.start()
        copies.append(copy)
    return copies


def k_early(pos, own, full, rest, sems):
    for copy in flush(pos[2], full, rest, sems, own, pos[0], pos[1]):
        copy.wait()


def k_final(pos, own, got, half, full, conv0, gain, bias, rest, sems):
    copies = flush(1 - pos[2], full, rest, sems, got, pos[1], pos[0])
    total = lift(own, 768) + lift(got, 768)
    conv0[...] = total[0:10]
    gain[...] = total[10:11]
    bias[...] = total[11:12]
    for copy in copies:
        copy.wait()


def where_am_i():
    dp, x = lax.axis_index("dp"), lax.axis_index("rep")
    core, y = lax.rem(dp, 2), lax.rem(lax.div(dp, 2), 4)
    first = jnp.where(core == 0, x, y)
    second = jnp.where(core == 0, y, x)
    return jnp.stack([first, second, core]).astype(jnp.int32)


def reduce_all(pos, other, mine, backward, feats):
    core, one, two, steps = perms()
    row = 512
    third = ((48, row), BF)
    got = send(other, core)
    own = mine(other)
    m1, m2, m3, keep = call(k_scatter_one, [((192, row), BF)] * 3 + [((192, row), F32)], [own, got], pos)
    r = [send(m, p) for m, p in zip((m1, m2, m3), one)]
    small = backward(0, 4, jnp.zeros((16, row), F32), keep)
    m1, m2, m3, keep2 = call(
        k_scatter_two, [third] * 3 + [((48, row), F32)], [keep, *r], pos, after=[small]
    )
    r = [send(m, p) for m, p in zip((m1, m2, m3), two)]
    small = backward(4, 2, small, keep2)
    (a,) = call(k_sum_two, [((80, row), BF)], [keep2, *r, small])
    for step in steps:
        b = send(a, step)
        (a,) = call(k_pair, [((80, row), BF)], [a, b])
    r = [send(a, p) for p in two]
    (a,) = call(k_join_two, [((224, row), BF)], [a, *r])
    feats = jnp.transpose(feats, (1, 0, 2))
    r = [send(a, p) for p in one]
    a, feats, *r = lax.optimization_barrier((a, feats, *r))
    (a,) = call(k_join_one, [((800, row), BF)], [a, *r])
    got = send(a, core)
    room = [pltpu.VMEM((768, row), F32), pltpu.SemaphoreType.DMA((4,))]
    grant = pltpu.CompilerParams(vmem_limit_bytes=20 << 20)
    whole = jax.ShapeDtypeStruct((1536, row), F32)
    half = pl.pallas_call(
        k_early, out_shape=whole, in_specs=[SM, VM], out_specs=ANY, scratch_shapes=room, compiler_params=grant
    )(pos, a)
    full, conv0, gain, bias = pl.pallas_call(
        k_final,
        out_shape=[whole] + [jax.ShapeDtypeStruct((n, row), F32) for n in (10, 1, 1)],
        in_specs=[SM, VM, VM, ANY],
        out_specs=[ANY, VM, VM, VM],
        scratch_shapes=room,
        input_output_aliases={3: 0},
        compiler_params=grant,
    )(pos, a, got, half)
    return full, conv0, gain[0], bias[0], jnp.transpose(feats, (1, 0, 2))


WIDE = 384


def k_pack(wave_in, length_in, target_in, out, rows, wave, length, target, sems):
    copies = [
        pltpu.make_async_copy(source, place, sems.at[n])
        for n, (source, place) in enumerate(((wave_in, wave), (length_in, length), (target_in, target)))
    ]
    for copy in copies:
        copy.start()
    for copy in copies:
        copy.wait()
    spans = wave.shape[0]
    goal = target[...].astype(F32)
    device = jnp.floor((goal + 0.5) * (1.0 / spans))
    slot = goal - device * spans
    up = lax.broadcasted_iota(jnp.int32, (spans, spans), 0)
    across = lax.broadcasted_iota(jnp.int32, (spans, spans), 1)

    def column(row):
        return jnp.sum(jnp.where(up == across, jnp.broadcast_to(row, (spans, spans)), 0.0), axis=1, keepdims=True)

    same = (column(device) == device) & (up < across)
    rank = jnp.sum(jnp.where(same, 1.0, 0.0), axis=0, keepdims=True)
    bucket = (device * 2.0 + rank).astype(jnp.int32)
    places = out.shape[0]
    pick = lax.broadcasted_iota(jnp.int32, (places, spans), 0) == bucket
    pick = jnp.where(pick, 1.0, 0.0).astype(BF)
    rows[...] = jnp.zeros(rows.shape, F32)
    rows[:, pl.ds(0, SAMPLES)] = wave[...].astype(F32)
    lane = lax.broadcasted_iota(jnp.int32, (spans, 128), 1)
    tail = rows[:, pl.ds(256, 128)]
    tail = jnp.where(lane == SAMPLES - 256, column(slot) + 1.0, tail)
    tail = jnp.where(lane == SAMPLES - 255, column(length[...].astype(F32)) - 214.0, tail)
    rows[:, pl.ds(256, 128)] = tail
    out[...] = jnp.dot(pick, rows[...].astype(BF), preferred_element_type=F32).astype(BF)


def gelu_parts(value):
    cumul = 0.5 * (1.0 + lax.erf(value * 0.7071067811865476))
    density = jnp.exp(-0.5 * value * value) * 0.3989422804014327
    return cumul, density


BLOCK = 8
ROWS = 32 * BLOCK


def k_taps(conv0, weo):
    taps = jnp.concatenate([conv0[...].astype(F32), jnp.zeros((6, 512), F32)], axis=0).astype(BF)
    weo[...] = jnp.zeros(weo.shape, BF)
    weo[pl.ds(0, 16), pl.ds(0, 512)] = taps
    weo[pl.ds(16, 16), pl.ds(512, 512)] = taps


def tables(fold, window):
    sample = lax.broadcasted_iota(jnp.int32, (WIDE, 128), 0).astype(F32)
    lane = lax.broadcasted_iota(jnp.int32, (WIDE, 128), 1).astype(F32)
    tens = jnp.floor((sample + 0.5) * 0.1) * 10.0
    fold[pl.ds(0, WIDE), :] = jnp.where((sample < SAMPLES) & (sample - tens == lane), 1.0, 0.0).astype(BF)
    tens = jnp.floor((sample - 4.5) * 0.1) * 10.0
    odd = (sample < SAMPLES) & (sample >= 5.0) & (sample - 5.0 - tens + 16.0 == lane)
    fold[pl.ds(WIDE, WIDE), :] = jnp.where(odd, 1.0, 0.0).astype(BF)
    step = lax.broadcasted_iota(jnp.int32, (32, WIDE), 0) * 10
    at = lax.broadcasted_iota(jnp.int32, (32, WIDE), 1)
    window[:, pl.ds(0, WIDE)] = jnp.where((at >= step) & (at < step + 10), 1.0, 0.0)
    window[:, pl.ds(WIDE, WIDE)] = jnp.where((at >= step + 5) & (at < step + 15), 1.0, 0.0)


def tall(rows):
    return jnp.concatenate([rows] * 4, axis=0)


def dot_t(left, right):
    return lax.dot_general(left, right, (((0,), (0,)), ((), ())), preferred_element_type=F32)


def dot_nt(left, right):
    return lax.dot_general(left, right, (((1,), (1,)), ((), ())), preferred_element_type=F32)


def k_forward(
    scale, pos, arrived, weo, gain, bias, weight, fgrad,
    feats, g, gs, se, so, ne, no, istd, valid, x, he, ho, other,
    fold, window, panels, am, pre, hs, pre1,
):
    spans = panels.shape[0]
    tables(fold, window)
    arr = arrived[...]
    lane = lax.broadcasted_iota(jnp.int32, (128, 128), 1).astype(F32)
    meta = arr[:, 256:384].astype(F32)
    slot = meta[:, SAMPLES - 256 : SAMPLES - 255]
    place = jnp.where(slot - 1.0 == lane, 1.0, 0.0).astype(BF)
    moved = dot_t(place, arr)[0:spans]
    panels[...] = jnp.broadcast_to(moved[:, None, :], panels.shape)
    length = moved[:, SAMPLES + 1 : SAMPLES + 2] + 214.0
    count = jnp.broadcast_to(jnp.floor((length - 9.5) * 0.2) + 1.0, (spans, 128))
    valid[...] = jnp.broadcast_to(count[:, None, :], valid.shape)
    frame = lax.broadcasted_iota(jnp.int32, (32, 128), 0).astype(F32)

    def block(b, carry):
        base = b * BLOCK

        def patch(q, carry):
            p = base + q
            count = tall(valid[p])
            keep_e, keep_o = 2.0 * frame < count, 2.0 * frame + 1.0 < count
            rows = pl.ds(pl.multiple_of(q * 32, 32), 32)
            for t in range(6):
                part = tall(panels[p, :, pl.ds((t % 3) * 128, 128)])
                part = jnp.where(keep_e if t < 3 else keep_o, part * window[:, pl.ds(t * 128, 128)], 0.0)
                am[rows, pl.ds(t * 128, 128)] = part.astype(BF)
            return carry

        lax.fori_loop(0, BLOCK, patch, 0, unroll=2)
        every = pl.ds(pl.multiple_of(b * ROWS, ROWS), ROWS)
        xs = jnp.dot(am[...], fold[...], preferred_element_type=F32).astype(BF)
        x[every, :] = xs
        pre[...] = jnp.dot(xs, weo[...], preferred_element_type=F32)

        def norm(q, carry):
            p = base + q
            count = valid[p]
            inverse = 1.0 / count[0:1]
            wide = tall(count)
            keep_e, keep_o = 2.0 * frame < wide, 2.0 * frame + 1.0 < wide
            rows = pl.ds(pl.multiple_of(q * 32, 32), 32)
            at = pl.ds(pl.multiple_of(p * 32, 32), 32)
            for t in range(4):
                cols = pl.ds(t * 128, 128)
                e = pre[rows, cols]
                o = pre[rows, pl.ds(512 + t * 128, 128)]
                center = jnp.sum(e + o, axis=0, keepdims=True) * inverse
                e = jnp.where(keep_e, e - center, 0.0)
                o = jnp.where(keep_o, o - center, 0.0)
                variance = jnp.sum(e * e + o * o, axis=0, keepdims=True) * inverse
                rs = lax.rsqrt(variance + 1e-05)
                istd[p, :, cols] = jnp.broadcast_to(rs, (8, 128))
                scale_row, bias_row = gain[:, cols], bias[:, cols]
                for value, keep, n_ref, s_ref, h_ref in ((e, keep_e, ne, se, he), (o, keep_o, no, so, ho)):
                    value = value * rs
                    n_ref[at, cols] = value.astype(BF)
                    value = value * scale_row + bias_row
                    cumul, density = gelu_parts(value)
                    hidden = jnp.where(keep, value * cumul, 0.0)
                    s_ref[at, cols] = jnp.where(keep, cumul + value * density, 0.0).astype(BF)
                    h_ref[at, cols] = hidden.astype(BF)
                    if h_ref is he:
                        hs[rows, cols] = pltpu.roll(hidden, 31, 0).astype(BF)
            return carry

        lax.fori_loop(0, BLOCK, norm, 0, unroll=2)
        pre1[...] = (
            jnp.dot(he[every, :], weight[0], preferred_element_type=F32)
            + jnp.dot(ho[every, :], weight[1], preferred_element_type=F32)
            + jnp.dot(hs[...], weight[2], preferred_element_type=F32)
        )

        def second(q, carry):
            p = base + q
            count = tall(jnp.floor((valid[p] - 2.5) * 0.5) + 1.0)
            keep = frame < count
            rows = pl.ds(pl.multiple_of(q * 32, 32), 32)
            at = pl.ds(pl.multiple_of(p * 32, 32), 32)
            for t in range(4):
                cols = pl.ds(t * 128, 128)
                value = pre1[rows, cols]
                cumul, density = gelu_parts(value)
                act = jnp.where(keep, value * cumul, 0.0)
                feats[p, :, cols] = act[0:31].astype(BF)
                up = fgrad[p, :, cols].astype(F32) * scale
                up = jnp.concatenate([up, jnp.zeros((1, 128), F32)], axis=0)
                grad = jnp.where(keep, up * (cumul + value * density), 0.0)
                g[at, cols] = grad.astype(BF)
                gs[at, cols] = pltpu.roll(grad, 1, 0).astype(BF)
            return carry

        lax.fori_loop(0, BLOCK, second, 0, unroll=2)
        return carry

    lax.fori_loop(0, spans // BLOCK, block, 0)
    half_of(1 - pos[2], he, ho, g, gs, other)


def half_of(half, he, ho, g, gs, out):
    @pl.when(half == 0)
    def _():
        out[pl.ds(0, 512), :] = dot_t(he[...], g[...]).astype(out.dtype)
        out[pl.ds(512, 256), :] = dot_t(ho[:, pl.ds(0, 256)], g[...]).astype(out.dtype)

    @pl.when(half == 1)
    def _():
        out[pl.ds(0, 256), :] = dot_t(ho[:, pl.ds(256, 256)], g[...]).astype(out.dtype)
        out[pl.ds(256, 512), :] = dot_t(he[...], gs[...]).astype(out.dtype)


def k_half(pos, he, ho, g, gs, before, out):
    half_of(pos[2], he, ho, g, gs, out)


def k_backward(
    first, g, gs, se, so, ne, no, istd, valid, x, gain, weight, start, before, small,
    de, do, dxe, dxo, sums,
):
    blocks = dxe.shape[0] // ROWS
    sums[...] = jnp.zeros(sums.shape, F32)

    def block(b, carry):
        base = (first + b) * BLOCK
        every = pl.ds(pl.multiple_of((first + b) * ROWS, ROWS), ROWS)
        de[...] = dot_nt(g[every, :], weight[0]) + dot_nt(gs[every, :], weight[2])
        do[...] = dot_nt(g[every, :], weight[1])

        def back(q, carry):
            p = base + q
            inverse = 1.0 / valid[p, pl.ds(0, 1), :]
            rows = pl.ds(pl.multiple_of(q * 32, 32), 32)
            at = pl.ds(pl.multiple_of(p * 32, 32), 32)
            here = pl.ds(pl.multiple_of((b * BLOCK + q) * 32, 32), 32)
            for t in range(4):
                cols = pl.ds(t * 128, 128)
                pe = de[rows, cols] * se[at, cols].astype(F32)
                po = do[rows, cols] * so[at, cols].astype(F32)
                e, o = ne[at, cols].astype(F32), no[at, cols].astype(F32)
                plain = jnp.sum(pe + po, axis=0, keepdims=True)
                mixed = jnp.sum(pe * e + po * o, axis=0, keepdims=True)
                sums[pl.ds(0, 1), cols] += mixed
                sums[pl.ds(1, 1), cols] += plain
                lead = istd[p, pl.ds(0, 1), cols] * gain[:, cols]
                plain, mixed = plain * inverse, mixed * inverse
                dxe[here, cols] = ((pe - plain - e * mixed) * lead).astype(BF)
                dxo[here, cols] = ((po - plain - o * mixed) * lead).astype(BF)
            return carry

        lax.fori_loop(0, BLOCK, back, 0, unroll=2)
        return carry

    lax.fori_loop(0, blocks, block, 0)
    part = x[pl.ds(first * ROWS, blocks * ROWS), :]
    small[...] = start[...] + dot_t(part, dxe[...])[0:16] + dot_t(part, dxo[...])[16:32]
    small[pl.ds(10, 2), :] += sums[pl.ds(0, 2), :]


def encode(pos, arrived, conv0_weight, norm_gain, norm_bias, conv1_weight, feature_grad, scale):
    spans = feature_grad.shape[0]
    rows = spans * 32
    (weo,) = call(k_taps, [((128, 1024), BF)], [conv0_weight])
    gain, bias = norm_gain[None], norm_bias[None]
    wide = ((rows, 512), BF)
    feats, g, gs, se, so, ne, no, istd, valid, x, he, ho, other = call(
        functools.partial(k_forward, scale),
        [
            (feature_grad.shape, BF), wide, wide, wide, wide, wide, wide,
            ((spans, 8, 512), F32), ((spans, 8, 128), F32), ((rows, 128), BF), wide, wide, ((768, 512), BF),
        ],
        [arrived, weo, gain, bias, conv1_weight, feature_grad],
        pos,
        scratch=[
            ((2 * WIDE, 128), BF), ((32, 2 * WIDE), F32), ((spans, 8, WIDE), F32), ((ROWS, 2 * WIDE), BF), ((ROWS, 1024), F32),
            ((ROWS, 512), BF), ((ROWS, 512), F32),
        ],
    )

    def mine(before):
        return call(k_half, [((768, 512), F32)], [he, ho, g, gs], pos, after=[before])[0]

    def backward(first, blocks, small, before):
        part = (ROWS * blocks, 512)
        return call(
            functools.partial(k_backward, first),
            [((16, 512), F32)],
            [g, gs, se, so, ne, no, istd, valid, x, gain, conv1_weight, small],
            scratch=[((ROWS, 512), F32), ((ROWS, 512), F32), (part, BF), (part, BF), ((8, 512), F32)],
            after=[before],
        )[0]

    return feats, other, mine, backward


def body(waveform, lengths, target, conv0_weight, norm_gain, norm_bias, conv1_weight, feature_grad):
    spans = waveform.shape[1]
    devices = lax.axis_size("dp")
    frames = feature_grad.shape[2]
    pos = where_am_i()
    (packed,) = call(
        k_pack,
        [((2 * devices, WIDE), BF)],
        [],
        scratch=[
            ((spans, WIDE), F32), (waveform.shape[1:], BF), (lengths.shape, jnp.int32), (target.shape, jnp.int32),
            pltpu.SemaphoreType.DMA((3,)),
        ],
        after=[waveform[0], lengths, target],
        late=HBM,
        limit=60,
    )
    arrived = lax.all_to_all(packed.reshape(devices, 2, WIDE), "dp", split_axis=0, concat_axis=0, tiled=True)
    arrived = arrived.reshape(2 * devices, WIDE)
    scale = 1.0 / float(lax.axis_size("rep") * devices * spans * frames) ** 0.5
    feats, other, mine, backward = encode(
        pos, arrived, conv0_weight, norm_gain, norm_bias, conv1_weight, feature_grad[0], scale
    )
    full, conv0, gain, bias, feats = reduce_all(pos, other, mine, backward, feats)
    return (feats[None], conv0, gain, bias, full.reshape(conv1_weight.shape))


def solution(mesh):
    placed = (
        P("rep", "dp", None),
        P("rep", "dp"),
        P("rep", "dp"),
        P(),
        P(),
        P(),
        P(),
        P("rep", "dp", None, None),
    )
    return jax.shard_map(
        body,
        mesh=mesh,
        in_specs=placed,
        out_specs=(P("rep", "dp", None, None), P(), P(), P(), P()),
        check_vma=False,
    )
```

```python
import functools

import jax
import jax.numpy as jnp
from jax import lax
from jax.experimental import pallas as pl
from jax.experimental.pallas import tpu as pltpu
from jax.sharding import PartitionSpec as P

BF, F32 = jnp.bfloat16, jnp.float32
VM = pl.BlockSpec(memory_space=pltpu.VMEM)
SM = pl.BlockSpec(memory_space=pltpu.SMEM)
ANY = pl.BlockSpec(memory_space=pl.ANY)
HBM = pl.BlockSpec(memory_space=pltpu.HBM)
BOTH = ("dp", "rep")
SAMPLES = 320


def call(kernel, outs, ins, scal=None, scratch=(), after=(), late=ANY, limit=20):
    specs = [VM] * len(ins) + [late] * len(after)
    ins = [*ins, *after]
    if scal is not None:
        specs = [SM] + specs
        ins = [scal, *ins]
    shapes = [jax.ShapeDtypeStruct(s, d) for s, d in outs]
    return pl.pallas_call(
        kernel,
        out_shape=shapes,
        in_specs=specs,
        out_specs=[VM] * len(outs),
        scratch_shapes=[pltpu.VMEM(*s) if isinstance(s, tuple) else s for s in scratch],
        compiler_params=pltpu.CompilerParams(vmem_limit_bytes=limit << 20),
    )(*ins)


def perms():
    every = [(z, y, c, x) for z in range(8) for y in range(4) for c in range(2) for x in range(4)]

    def lin(z, y, c, x):
        return ((z * 4 + y) * 2 + c) * 4 + x

    def build(move):
        return [(lin(*p), lin(*move(*p))) for p in every]

    def along(first, k):
        def move(z, y, c, x):
            if (c == 0) == first:
                return (z, y, c, (x + k) % 4)
            return (z, (y + k) % 4, c, x)

        return build(move)

    core = build(lambda z, y, c, x: (z, y, 1 - c, x))
    one = [along(True, k) for k in range(1, 4)]
    two = [along(False, k) for k in range(1, 4)]
    steps = [build(lambda z, y, c, x, flip=flip: (z ^ flip, y, c, x)) for flip in (1, 3, 7)]
    return core, one, two, steps


def send(value, perm):
    return lax.ppermute(value, BOTH, perm)


def k_scatter_one(pos, own, got, m1, m2, m3, keep):
    a1 = pos[0]
    for k, out in ((0, None), (1, m1), (2, m2), (3, m3)):
        j = (a1 + k) & 3
        rows = pl.ds(pl.multiple_of(j * 192, 192), 192)
        total = own[rows, :] + got[rows, :].astype(F32)
        if out is None:
            keep[...] = total
        else:
            out[...] = total.astype(BF)


def k_scatter_two(pos, keep, r1, r2, r3, before, m1, m2, m3, keep2):
    a2 = pos[1]
    for k, out in ((0, None), (1, m1), (2, m2), (3, m3)):
        rows = pl.ds(pl.multiple_of(((a2 + k) & 3) * 48, 16), 48)
        total = keep[rows, :] + r1[rows, :].astype(F32) + r2[rows, :].astype(F32) + r3[rows, :].astype(F32)
        if out is None:
            keep2[...] = total
        else:
            out[...] = total.astype(BF)


def lift(ref, at):
    return ref[pl.ds(at, 16), :].astype(F32) + ref[pl.ds(at + 16, 16), :].astype(F32)


def put(out, at, value):
    high = value.astype(BF)
    out[pl.ds(at, 16), :] = high
    out[pl.ds(at + 16, 16), :] = (value - high.astype(F32)).astype(BF)


def k_sum_two(keep2, r1, r2, r3, small, out):
    out[pl.ds(0, 48), :] = (
        (keep2[...] + r2[...].astype(F32)) + (r1[...].astype(F32) + r3[...].astype(F32))
    ).astype(BF)
    put(out, 48, small[...])


def k_pair(a, b, *rest):
    out = rest[-1]
    head = pl.ds(0, 48)
    out[head, :] = (a[head, :].astype(F32) + b[head, :].astype(F32)).astype(BF)
    put(out, 48, lift(a, 48) + lift(b, 48))


def k_join_two(own, r1, r2, r3, out):
    for k, part in enumerate((own, r1, r2, r3)):
        out[pl.ds(48 * k, 48), :] = part[pl.ds(0, 48), :]
    put(out, 192, (lift(own, 48) + lift(r2, 48)) + (lift(r1, 48) + lift(r3, 48)))


def k_join_one(own, r1, r2, r3, out):
    for k, part in enumerate((own, r1, r2, r3)):
        out[pl.ds(192 * k, 192), :] = part[pl.ds(0, 192), :]
    put(out, 768, (lift(own, 192) + lift(r2, 192)) + (lift(r1, 192) + lift(r3, 192)))


def order(ref, out, j1, first, second):
    for j2 in range(4):
        at = ((first - j1) & 3) * 4 + ((second - j2) & 3)
        out[pl.ds((j1 * 4 + j2) * 48, 48), :] = ref[pl.ds(pl.multiple_of(at * 48, 16), 48), :].astype(F32)


def flush(core, out, rest, sems, ref, first, second):
    copies = []
    for j1 in range(4):
        order(ref, rest, j1, first, second)
        at = pl.multiple_of(core * 768 + j1 * 192, 192)
        copy = pltpu.make_async_copy(rest.at[pl.ds(j1 * 192, 192), :], out.at[pl.ds(at, 192), :], sems.at[j1])
        copy.start()
        copies.append(copy)
    return copies


def k_early(pos, own, full, rest, sems):
    for copy in flush(pos[2], full, rest, sems, own, pos[0], pos[1]):
        copy.wait()


def k_final(pos, own, got, half, full, conv0, gain, bias, rest, sems):
    copies = flush(1 - pos[2], full, rest, sems, got, pos[1], pos[0])
    total = lift(own, 768) + lift(got, 768)
    conv0[...] = total[0:10]
    gain[...] = total[10:11]
    bias[...] = total[11:12]
    for copy in copies:
        copy.wait()


def where_am_i():
    dp, x = lax.axis_index("dp"), lax.axis_index("rep")
    core, y = lax.rem(dp, 2), lax.rem(lax.div(dp, 2), 4)
    first = jnp.where(core == 0, x, y)
    second = jnp.where(core == 0, y, x)
    return jnp.stack([first, second, core]).astype(jnp.int32)


def reduce_all(pos, other, mine, backward, features):
    core, one, two, steps = perms()
    row = 512
    third = ((48, row), BF)
    got = send(other, core)
    own = mine(other)
    m1, m2, m3, keep = call(k_scatter_one, [((192, row), BF)] * 3 + [((192, row), F32)], [own, got], pos)
    r = [send(m, p) for m, p in zip((m1, m2, m3), one)]
    small = backward(0, 2, jnp.zeros((16, row), F32), keep)
    m1, m2, m3, keep2 = call(
        k_scatter_two, [third] * 3 + [((48, row), F32)], [keep, *r], pos, after=[small]
    )
    r = [send(m, p) for m, p in zip((m1, m2, m3), two)]
    small = backward(2, 1, small, keep2)
    (a,) = call(k_sum_two, [((80, row), BF)], [keep2, *r, small])
    feats = None
    for n, step in enumerate(steps):
        b = send(a, step)
        if n == 1:
            feats, token = features(a)
        (a,) = call(k_pair, [((80, row), BF)], [a, b], after=[token] if n == 1 else [])
    r = [send(a, p) for p in two]
    (a,) = call(k_join_two, [((224, row), BF)], [a, *r])
    r = [send(a, p) for p in one]
    (a,) = call(k_join_one, [((800, row), BF)], [a, *r])
    got = send(a, core)
    room = [pltpu.VMEM((768, row), F32), pltpu.SemaphoreType.DMA((4,))]
    grant = pltpu.CompilerParams(vmem_limit_bytes=20 << 20)
    whole = jax.ShapeDtypeStruct((1536, row), F32)
    half = pl.pallas_call(
        k_early, out_shape=whole, in_specs=[SM, VM], out_specs=ANY, scratch_shapes=room, compiler_params=grant
    )(pos, a)
    full, conv0, gain, bias = pl.pallas_call(
        k_final,
        out_shape=[whole] + [jax.ShapeDtypeStruct((n, row), F32) for n in (10, 1, 1)],
        in_specs=[SM, VM, VM, ANY],
        out_specs=[ANY, VM, VM, VM],
        scratch_shapes=room,
        input_output_aliases={3: 0},
        compiler_params=grant,
    )(pos, a, got, half)
    return full, conv0, gain[0], bias[0], jnp.transpose(feats, (1, 0, 2))


WIDE = 384


def k_pack(wave_in, length_in, target_in, out, rows, wave, length, target, sems):
    copies = [
        pltpu.make_async_copy(source, place, sems.at[n])
        for n, (source, place) in enumerate(((wave_in, wave), (length_in, length), (target_in, target)))
    ]
    for copy in copies:
        copy.start()
    for copy in copies:
        copy.wait()
    spans = wave.shape[0]
    goal = target[...].astype(F32)
    device = jnp.floor((goal + 0.5) * (1.0 / spans))
    slot = goal - device * spans
    up = lax.broadcasted_iota(jnp.int32, (spans, spans), 0)
    across = lax.broadcasted_iota(jnp.int32, (spans, spans), 1)

    def column(row):
        return jnp.sum(jnp.where(up == across, jnp.broadcast_to(row, (spans, spans)), 0.0), axis=1, keepdims=True)

    same = (column(device) == device) & (up < across)
    rank = jnp.sum(jnp.where(same, 1.0, 0.0), axis=0, keepdims=True)
    bucket = (device * 2.0 + rank).astype(jnp.int32)
    places = out.shape[0] * out.shape[1]
    pick = lax.broadcasted_iota(jnp.int32, (places, spans), 0) == bucket
    pick = jnp.where(pick, 1.0, 0.0).astype(BF)
    rows[...] = jnp.zeros(rows.shape, F32)
    rows[:, pl.ds(0, SAMPLES)] = wave[...].astype(F32)
    lane = lax.broadcasted_iota(jnp.int32, (spans, 128), 1)
    tail = rows[:, pl.ds(256, 128)]
    tail = jnp.where(lane == SAMPLES - 256, column(slot) + 1.0, tail)
    tail = jnp.where(lane == SAMPLES - 255, column(length[...].astype(F32)) - 214.0, tail)
    rows[:, pl.ds(256, 128)] = tail
    packed = jnp.dot(pick, rows[...].astype(BF), preferred_element_type=F32)
    out[...] = packed.reshape(out.shape).astype(BF)


def gelu_parts(value):
    cumul = 0.5 * (1.0 + lax.erf(value * 0.7071067811865476))
    density = jnp.exp(-0.5 * value * value) * 0.3989422804014327
    return cumul, density


BLOCK = 8
BACK = 16
ROWS = 32 * BLOCK


def k_taps(conv0, weo):
    taps = jnp.concatenate([conv0[...].astype(F32), jnp.zeros((6, 512), F32)], axis=0).astype(BF)
    weo[...] = jnp.zeros(weo.shape, BF)
    weo[pl.ds(0, 16), pl.ds(0, 512)] = taps
    weo[pl.ds(16, 16), pl.ds(512, 512)] = taps


def tables(fold, window):
    sample = lax.broadcasted_iota(jnp.int32, (256, 128), 0).astype(F32)
    lane = lax.broadcasted_iota(jnp.int32, (256, 128), 1).astype(F32)
    tens = jnp.floor((sample + 0.5) * 0.1) * 10.0
    fold[pl.ds(0, 256), :] = jnp.where(sample - tens == lane, 1.0, 0.0).astype(BF)
    tens = jnp.floor((sample - 4.5) * 0.1) * 10.0
    odd = (sample >= 5.0) & (sample - 5.0 - tens + 16.0 == lane)
    fold[pl.ds(256, 256), :] = jnp.where(odd, 1.0, 0.0).astype(BF)
    step = lax.broadcasted_iota(jnp.int32, (32, 256), 0)
    step = jnp.where(step < 16, step, step - 16) * 10
    at = lax.broadcasted_iota(jnp.int32, (32, 256), 1)
    window[:, pl.ds(0, 256)] = jnp.where((at >= step) & (at < step + 10), 1.0, 0.0)
    window[:, pl.ds(256, 256)] = jnp.where((at >= step + 5) & (at < step + 15), 1.0, 0.0)


def tall(rows):
    return jnp.concatenate([rows] * 4, axis=0)


def dot_t(left, right):
    return lax.dot_general(left, right, (((0,), (0,)), ((), ())), preferred_element_type=F32)


def dot_nt(left, right):
    return lax.dot_general(left, right, (((1,), (1,)), ((), ())), preferred_element_type=F32)


def k_forward(
    scale, pos, arrived, weo, gain, bias, weight, fgrad,
    pre1, second_count, g, gs, se, so, ne, no, istd, valid, x, he, ho, other,
    fold, window, panels, am, pre, hs,
):
    spans = panels.shape[0]
    tables(fold, window)
    arr = arrived[...]
    lane = lax.broadcasted_iota(jnp.int32, (128, 128), 1).astype(F32)
    meta = arr[:, 256:384].astype(F32)
    slot = meta[:, SAMPLES - 256 : SAMPLES - 255]
    place = jnp.where(slot - 1.0 == lane, 1.0, 0.0).astype(BF)
    moved = dot_t(place, arr)[0:spans]
    late = pltpu.roll(moved, WIDE - 160, 1)
    both = jnp.concatenate([moved[:, 0:256], late[:, 0:256]], axis=1)
    panels[...] = jnp.broadcast_to(both[:, None, :], panels.shape)
    length = moved[:, SAMPLES + 1 : SAMPLES + 2] + 214.0
    count = jnp.broadcast_to(jnp.floor((length - 9.5) * 0.2) + 1.0, (spans, 128))
    valid[...] = jnp.broadcast_to(count[:, None, :], valid.shape)
    second_count[...] = jnp.floor((count - 2.5) * 0.5) + 1.0
    frame = lax.broadcasted_iota(jnp.int32, (32, 128), 0).astype(F32)

    def block(b, carry):
        base = b * BLOCK

        def patch(q, carry):
            p = base + q
            count = tall(valid[p])
            keep_e, keep_o = 2.0 * frame < count, 2.0 * frame + 1.0 < count
            rows = pl.ds(pl.multiple_of(q * 32, 32), 32)
            for t in range(4):
                early = panels[p, :, pl.ds((t % 2) * 128, 128)]
                late = panels[p, :, pl.ds(256 + (t % 2) * 128, 128)]
                part = jnp.concatenate([early, early, late, late], axis=0)
                part = jnp.where(keep_e if t < 2 else keep_o, part * window[:, pl.ds(t * 128, 128)], 0.0)
                am[rows, pl.ds(t * 128, 128)] = part.astype(BF)
            return carry

        lax.fori_loop(0, BLOCK, patch, 0, unroll=2)
        every = pl.ds(pl.multiple_of(b * ROWS, ROWS), ROWS)
        xs = jnp.dot(am[...], fold[...], preferred_element_type=F32).astype(BF)
        x[every, :] = xs
        pre[...] = jnp.dot(xs, weo[...], preferred_element_type=F32)

        def norm(q, carry):
            p = base + q
            count = valid[p]
            inverse = 1.0 / count[0:1]
            wide = tall(count)
            keep_e, keep_o = 2.0 * frame < wide, 2.0 * frame + 1.0 < wide
            rows = pl.ds(pl.multiple_of(q * 32, 32), 32)
            at = pl.ds(pl.multiple_of(p * 32, 32), 32)
            for t in range(4):
                cols = pl.ds(t * 128, 128)
                e = pre[rows, cols]
                o = pre[rows, pl.ds(512 + t * 128, 128)]
                center = jnp.sum(e + o, axis=0, keepdims=True) * inverse
                e = jnp.where(keep_e, e - center, 0.0)
                o = jnp.where(keep_o, o - center, 0.0)
                variance = jnp.sum(e * e + o * o, axis=0, keepdims=True) * inverse
                rs = lax.rsqrt(variance + 1e-05)
                istd[p, :, cols] = jnp.broadcast_to(rs, (8, 128))
                scale_row, bias_row = gain[:, cols], bias[:, cols]
                for value, keep, n_ref, s_ref, h_ref in ((e, keep_e, ne, se, he), (o, keep_o, no, so, ho)):
                    value = value * rs
                    n_ref[at, cols] = value.astype(BF)
                    value = value * scale_row + bias_row
                    cumul, density = gelu_parts(value)
                    hidden = jnp.where(keep, value * cumul, 0.0)
                    s_ref[at, cols] = jnp.where(keep, cumul + value * density, 0.0).astype(BF)
                    h_ref[at, cols] = hidden.astype(BF)
                    if h_ref is he:
                        hs[rows, cols] = pltpu.roll(hidden, 31, 0).astype(BF)
            return carry

        lax.fori_loop(0, BLOCK, norm, 0, unroll=2)
        total = (
            jnp.dot(he[every, :], weight[0], preferred_element_type=F32)
            + jnp.dot(ho[every, :], weight[1], preferred_element_type=F32)
            + jnp.dot(hs[...], weight[2], preferred_element_type=F32)
        )
        for t in range(4):
            pre1[t, every, :] = total[:, t * 128 : t * 128 + 128]

        def second(q, carry):
            p = base + q
            count = tall(jnp.floor((valid[p] - 2.5) * 0.5) + 1.0)
            keep = frame < count
            at = pl.ds(pl.multiple_of(p * 32, 32), 32)
            for t in range(4):
                cols = pl.ds(t * 128, 128)
                value = pre1[t, at, :]
                cumul, density = gelu_parts(value)
                up = fgrad[p, :, cols].astype(F32) * scale
                up = jnp.concatenate([up, jnp.zeros((1, 128), F32)], axis=0)
                grad = jnp.where(keep, up * (cumul + value * density), 0.0)
                g[at, cols] = grad.astype(BF)
                gs[at, cols] = pltpu.roll(grad, 1, 0).astype(BF)
            return carry

        lax.fori_loop(0, BLOCK, second, 0, unroll=2)
        return carry

    lax.fori_loop(0, spans // BLOCK, block, 0)
    half_of(1 - pos[2], he, ho, g, gs, other)


def half_of(half, he, ho, g, gs, out):
    @pl.when(half == 0)
    def _():
        out[pl.ds(0, 512), :] = dot_t(he[...], g[...]).astype(out.dtype)
        out[pl.ds(512, 256), :] = dot_t(ho[:, pl.ds(0, 256)], g[...]).astype(out.dtype)

    @pl.when(half == 1)
    def _():
        out[pl.ds(0, 256), :] = dot_t(ho[:, pl.ds(256, 256)], g[...]).astype(out.dtype)
        out[pl.ds(256, 512), :] = dot_t(he[...], gs[...]).astype(out.dtype)


def k_half(pos, he, ho, g, gs, before, out):
    half_of(pos[2], he, ho, g, gs, out)


def k_features(pre1, count, before, feats, token):
    token[...] = jnp.zeros(token.shape, F32)
    spans = count.shape[0]

    def frame(t, carry):
        keep = count[...] > lax.convert_element_type(t, F32)
        for c in range(4):
            cols = pl.ds(c * 128, 128)
            value = pre1[c, pl.ds(t, spans, stride=32), :]
            cumul, _ = gelu_parts(value)
            feats[t, :, cols] = jnp.where(keep, value * cumul, 0.0).astype(BF)
        return carry

    lax.fori_loop(0, feats.shape[0], frame, 0)


def k_backward(
    first, g, gs, se, so, ne, no, istd, valid, x, gain, weight, start, before, small,
    de, do, dxe, dxo, sums,
):
    blocks = dxe.shape[0] // (32 * BACK)
    sums[...] = jnp.zeros(sums.shape, F32)

    def block(b, carry):
        base = (first + b) * BACK
        every = pl.ds(pl.multiple_of((first + b) * (32 * BACK), (32 * BACK)), (32 * BACK))
        de[...] = dot_nt(g[every, :], weight[0]) + dot_nt(gs[every, :], weight[2])
        do[...] = dot_nt(g[every, :], weight[1])

        def back(q, carry):
            p = base + q
            inverse = 1.0 / valid[p, pl.ds(0, 1), :]
            rows = pl.ds(pl.multiple_of(q * 32, 32), 32)
            at = pl.ds(pl.multiple_of(p * 32, 32), 32)
            here = pl.ds(pl.multiple_of((b * BACK + q) * 32, 32), 32)
            for t in range(4):
                cols = pl.ds(t * 128, 128)
                pe = de[rows, cols] * se[at, cols].astype(F32)
                po = do[rows, cols] * so[at, cols].astype(F32)
                e, o = ne[at, cols].astype(F32), no[at, cols].astype(F32)
                plain = jnp.sum(pe + po, axis=0, keepdims=True)
                mixed = jnp.sum(pe * e + po * o, axis=0, keepdims=True)
                sums[pl.ds(0, 1), cols] += mixed
                sums[pl.ds(1, 1), cols] += plain
                lead = istd[p, pl.ds(0, 1), cols] * gain[:, cols]
                plain, mixed = plain * inverse, mixed * inverse
                dxe[here, cols] = ((pe - plain - e * mixed) * lead).astype(BF)
                dxo[here, cols] = ((po - plain - o * mixed) * lead).astype(BF)
            return carry

        lax.fori_loop(0, BACK, back, 0, unroll=2)
        return carry

    lax.fori_loop(0, blocks, block, 0)
    part = x[pl.ds(first * (32 * BACK), blocks * (32 * BACK)), :]
    small[...] = start[...] + dot_t(part, dxe[...])[0:16] + dot_t(part, dxo[...])[16:32]
    small[pl.ds(10, 2), :] += sums[pl.ds(0, 2), :]


def encode(pos, arrived, conv0_weight, norm_gain, norm_bias, conv1_weight, feature_grad, scale):
    spans = feature_grad.shape[0]
    rows = spans * 32
    (weo,) = call(k_taps, [((128, 1024), BF)], [conv0_weight])
    gain, bias = norm_gain[None], norm_bias[None]
    wide = ((rows, 512), BF)
    pre1, count, g, gs, se, so, ne, no, istd, valid, x, he, ho, other = call(
        functools.partial(k_forward, scale),
        [
            ((4, rows, 128), F32), ((spans, 128), F32), wide, wide, wide, wide, wide, wide,
            ((spans, 8, 512), F32), ((spans, 8, 128), F32), ((rows, 128), BF), wide, wide, ((768, 512), BF),
        ],
        [arrived, weo, gain, bias, conv1_weight, feature_grad],
        pos,
        scratch=[
            ((512, 128), BF), ((32, 512), F32), ((spans, 8, 512), F32), ((ROWS, 512), BF), ((ROWS, 1024), F32),
            ((ROWS, 512), BF),
        ],
    )

    def features(before):
        frames = feature_grad.shape[1]
        return call(
            k_features, [((frames, spans, 512), BF), ((8, 128), F32)], [pre1, count], after=[before]
        )

    def mine(before):
        return call(k_half, [((768, 512), F32)], [he, ho, g, gs], pos, after=[before])[0]

    def backward(first, blocks, small, before):
        part, step = (32 * BACK * blocks, 512), (32 * BACK, 512)
        return call(
            functools.partial(k_backward, first),
            [((16, 512), F32)],
            [g, gs, se, so, ne, no, istd, valid, x, gain, conv1_weight, small],
            scratch=[(step, F32), (step, F32), (part, BF), (part, BF), ((8, 512), F32)],
            after=[before],
        )[0]

    return features, other, mine, backward


def body(waveform, lengths, target, conv0_weight, norm_gain, norm_bias, conv1_weight, feature_grad):
    spans = waveform.shape[1]
    devices = lax.axis_size("dp")
    frames = feature_grad.shape[2]
    pos = where_am_i()
    (packed,) = call(
        k_pack,
        [((devices, 2, WIDE), BF)],
        [],
        scratch=[
            ((spans, WIDE), F32), (waveform.shape[1:], BF), (lengths.shape, jnp.int32), (target.shape, jnp.int32),
            pltpu.SemaphoreType.DMA((3,)),
        ],
        after=[waveform[0], lengths, target],
        late=HBM,
        limit=60,
    )
    arrived = lax.all_to_all(packed, "dp", split_axis=0, concat_axis=0, tiled=True)
    arrived = arrived.reshape(2 * devices, WIDE)
    scale = 1.0 / float(lax.axis_size("rep") * devices * spans * frames) ** 0.5
    features, other, mine, backward = encode(
        pos, arrived, conv0_weight, norm_gain, norm_bias, conv1_weight, feature_grad[0], scale
    )
    full, conv0, gain, bias, feats = reduce_all(pos, other, mine, backward, features)
    return (feats[None], conv0, gain, bias, full.reshape(conv1_weight.shape))


def solution(mesh):
    placed = (
        P("rep", "dp", None),
        P("rep", "dp"),
        P("rep", "dp"),
        P(),
        P(),
        P(),
        P(),
        P("rep", "dp", None, None),
    )
    return jax.shard_map(
        body,
        mesh=mesh,
        in_specs=placed,
        out_specs=(P("rep", "dp", None, None), P(), P(), P(), P()),
        check_vma=False,
    )
```

```python
import functools

import jax
import jax.numpy as jnp
from jax import lax
from jax.experimental import pallas as pl
from jax.experimental.pallas import tpu as pltpu
from jax.sharding import PartitionSpec as P

BF, F32 = jnp.bfloat16, jnp.float32
VM = pl.BlockSpec(memory_space=pltpu.VMEM)
SM = pl.BlockSpec(memory_space=pltpu.SMEM)
ANY = pl.BlockSpec(memory_space=pl.ANY)
HBM = pl.BlockSpec(memory_space=pltpu.HBM)
BOTH = ("dp", "rep")
SAMPLES = 320


def call(kernel, outs, ins, scal=None, scratch=(), after=(), late=ANY, limit=20):
    specs = [VM] * len(ins) + [late] * len(after)
    ins = [*ins, *after]
    if scal is not None:
        specs = [SM] + specs
        ins = [scal, *ins]
    shapes = [jax.ShapeDtypeStruct(s, d) for s, d in outs]
    return pl.pallas_call(
        kernel,
        out_shape=shapes,
        in_specs=specs,
        out_specs=[VM] * len(outs),
        scratch_shapes=[pltpu.VMEM(*s) if isinstance(s, tuple) else s for s in scratch],
        compiler_params=pltpu.CompilerParams(vmem_limit_bytes=limit << 20),
    )(*ins)


def perms():
    every = [(z, y, c, x) for z in range(8) for y in range(4) for c in range(2) for x in range(4)]

    def lin(z, y, c, x):
        return ((z * 4 + y) * 2 + c) * 4 + x

    def build(move):
        return [(lin(*p), lin(*move(*p))) for p in every]

    def along(first, k):
        def move(z, y, c, x):
            if (c == 1) == first:
                return (z, y, c, (x + k) % 4)
            return (z, (y + k) % 4, c, x)

        return build(move)

    core = build(lambda z, y, c, x: (z, y, 1 - c, x))
    one = [along(True, k) for k in range(1, 4)]
    two = [along(False, k) for k in range(1, 4)]
    steps = [build(lambda z, y, c, x, flip=flip: (z ^ flip, y, c, x)) for flip in (1, 3, 7)]
    return core, one, two, steps


def send(value, perm):
    return lax.ppermute(value, BOTH, perm)


def k_scatter_one(pos, own, got, m1, m2, m3, keep):
    a1 = pos[0]
    for k, out in ((0, None), (1, m1), (2, m2), (3, m3)):
        j = (a1 + k) & 3
        rows = pl.ds(pl.multiple_of(j * 192, 192), 192)
        total = own[rows, :] + got[rows, :].astype(F32)
        if out is None:
            keep[...] = total
        else:
            out[...] = total.astype(BF)


def k_scatter_two(pos, keep, r1, r2, r3, before, m1, m2, m3, keep2):
    a2 = pos[1]
    for k, out in ((0, None), (1, m1), (2, m2), (3, m3)):
        rows = pl.ds(pl.multiple_of(((a2 + k) & 3) * 48, 16), 48)
        total = keep[rows, :] + r1[rows, :].astype(F32) + r2[rows, :].astype(F32) + r3[rows, :].astype(F32)
        if out is None:
            keep2[...] = total
        else:
            out[...] = total.astype(BF)


def lift(ref, at):
    return ref[pl.ds(at, 16), :].astype(F32) + ref[pl.ds(at + 16, 16), :].astype(F32)


def put(out, at, value):
    high = value.astype(BF)
    out[pl.ds(at, 16), :] = high
    out[pl.ds(at + 16, 16), :] = (value - high.astype(F32)).astype(BF)


def k_sum_two(keep2, r1, r2, r3, small, out):
    out[pl.ds(0, 48), :] = (
        (keep2[...] + r2[...].astype(F32)) + (r1[...].astype(F32) + r3[...].astype(F32))
    ).astype(BF)
    put(out, 48, small[...])


def k_pair(a, b, *rest):
    out = rest[-1]
    head = pl.ds(0, 48)
    out[head, :] = (a[head, :].astype(F32) + b[head, :].astype(F32)).astype(BF)
    put(out, 48, lift(a, 48) + lift(b, 48))


def k_join_two(own, r1, r2, r3, out):
    for k, part in enumerate((own, r1, r2, r3)):
        out[pl.ds(48 * k, 48), :] = part[pl.ds(0, 48), :]
    put(out, 192, (lift(own, 48) + lift(r2, 48)) + (lift(r1, 48) + lift(r3, 48)))


def k_join_one(own, r1, r2, r3, out):
    for k, part in enumerate((own, r1, r2, r3)):
        out[pl.ds(192 * k, 192), :] = part[pl.ds(0, 192), :]
    put(out, 768, (lift(own, 192) + lift(r2, 192)) + (lift(r1, 192) + lift(r3, 192)))


def order(ref, out, j1, first, second):
    for j2 in range(4):
        at = ((first - j1) & 3) * 4 + ((second - j2) & 3)
        out[pl.ds((j1 * 4 + j2) * 48, 48), :] = ref[pl.ds(pl.multiple_of(at * 48, 16), 48), :].astype(F32)


def flush(core, out, rest, sems, ref, first, second):
    copies = []
    for j1 in range(4):
        order(ref, rest, j1, first, second)
        at = pl.multiple_of(core * 768 + j1 * 192, 192)
        copy = pltpu.make_async_copy(rest.at[pl.ds(j1 * 192, 192), :], out.at[pl.ds(at, 192), :], sems.at[j1])
        copy.start()
        copies.append(copy)
    return copies


def k_early(pos, own, full, rest, sems):
    for copy in flush(pos[2], full, rest, sems, own, pos[0], pos[1]):
        copy.wait()


def k_final(pos, own, got, half, full, conv0, gain, bias, rest, sems, conv0_row, gain_row, bias_row, small_sems):
    total = lift(own, 768) + lift(got, 768)
    conv0_row[...] = total[0:10]
    gain_row[...] = total[10:11]
    bias_row[...] = total[11:12]
    copies = [
        pltpu.make_async_copy(source, out, small_sems.at[n])
        for n, (source, out) in enumerate(((conv0_row, conv0), (gain_row, gain), (bias_row, bias)))
    ]
    for copy in copies:
        copy.start()
    copies += flush(1 - pos[2], full, rest, sems, got, pos[1], pos[0])
    for copy in copies:
        copy.wait()


def where_am_i():
    dp, x = lax.axis_index("dp"), lax.axis_index("rep")
    core, y = lax.rem(dp, 2), lax.rem(lax.div(dp, 2), 4)
    first = jnp.where(core == 0, y, x)
    second = jnp.where(core == 0, x, y)
    return jnp.stack([first, second, core]).astype(jnp.int32)


def reduce_all(pos, other, mine, backward, features):
    core, one, two, steps = perms()
    row = 512
    third = ((48, row), BF)
    got = send(other, core)
    own = mine(other)
    m1, m2, m3, keep = call(k_scatter_one, [((192, row), BF)] * 3 + [((192, row), F32)], [own, got], pos)
    r = [send(m, p) for m, p in zip((m1, m2, m3), one)]
    small = backward(0, 2, jnp.zeros((16, row), F32), keep)
    m1, m2, m3, keep2 = call(
        k_scatter_two, [third] * 3 + [((48, row), F32)], [keep, *r], pos, after=[small]
    )
    r = [send(m, p) for m, p in zip((m1, m2, m3), two)]
    small = backward(2, 1, small, keep2)
    (a,) = call(k_sum_two, [((80, row), BF)], [keep2, *r, small])
    feats = None
    for n, step in enumerate(steps):
        b = send(a, step)
        if n == 1:
            feats, token = features(a)
        (a,) = call(k_pair, [((80, row), BF)], [a, b], after=[token] if n == 1 else [])
    r = [send(a, p) for p in two]
    (a,) = call(k_join_two, [((224, row), BF)], [a, *r])
    r = [send(a, p) for p in one]
    (a,) = call(k_join_one, [((800, row), BF)], [a, *r])
    got = send(a, core)
    room = [pltpu.VMEM((768, row), F32), pltpu.SemaphoreType.DMA((4,))]
    grant = pltpu.CompilerParams(vmem_limit_bytes=20 << 20)
    whole = jax.ShapeDtypeStruct((1536, row), F32)
    half = pl.pallas_call(
        k_early, out_shape=whole, in_specs=[SM, VM], out_specs=ANY, scratch_shapes=room, compiler_params=grant
    )(pos, a)
    full, conv0, gain, bias = pl.pallas_call(
        k_final,
        out_shape=[whole] + [jax.ShapeDtypeStruct((n, row), F32) for n in (10, 1, 1)],
        in_specs=[SM, VM, VM, ANY],
        out_specs=[ANY] * 4,
        scratch_shapes=[*room, *(pltpu.VMEM((n, row), F32) for n in (10, 1, 1)), pltpu.SemaphoreType.DMA((3,))],
        input_output_aliases={3: 0},
        compiler_params=grant,
    )(pos, a, got, half)
    return full, conv0, gain[0], bias[0], jnp.transpose(feats, (1, 0, 2))


WIDE = 384


def k_pack(wave_in, length_in, target_in, out, rows, wave, length, target, sems):
    copies = [
        pltpu.make_async_copy(source, place, sems.at[n])
        for n, (source, place) in enumerate(((wave_in, wave), (length_in, length), (target_in, target)))
    ]
    for copy in copies:
        copy.start()
    for copy in copies:
        copy.wait()
    spans = wave.shape[0]
    goal = target[...].astype(F32)
    device = jnp.floor((goal + 0.5) * (1.0 / spans))
    slot = goal - device * spans
    up = lax.broadcasted_iota(jnp.int32, (spans, spans), 0)
    across = lax.broadcasted_iota(jnp.int32, (spans, spans), 1)

    def column(row):
        return jnp.sum(jnp.where(up == across, jnp.broadcast_to(row, (spans, spans)), 0.0), axis=1, keepdims=True)

    same = (column(device) == device) & (up < across)
    rank = jnp.sum(jnp.where(same, 1.0, 0.0), axis=0, keepdims=True)
    bucket = (device * 2.0 + rank).astype(jnp.int32)
    places = out.shape[0] * out.shape[1]
    pick = lax.broadcasted_iota(jnp.int32, (places, spans), 0) == bucket
    pick = jnp.where(pick, 1.0, 0.0).astype(BF)
    rows[...] = jnp.zeros(rows.shape, F32)
    rows[:, pl.ds(0, SAMPLES)] = wave[...].astype(F32)
    lane = lax.broadcasted_iota(jnp.int32, (spans, 128), 1)
    tail = rows[:, pl.ds(256, 128)]
    tail = jnp.where(lane == SAMPLES - 256, column(slot) + 1.0, tail)
    tail = jnp.where(lane == SAMPLES - 255, column(length[...].astype(F32)) - 214.0, tail)
    rows[:, pl.ds(256, 128)] = tail
    packed = jnp.dot(pick, rows[...].astype(BF), preferred_element_type=F32)
    out[...] = packed.reshape(out.shape).astype(BF)


def gelu_parts(value):
    cumul = 0.5 * (1.0 + lax.erf(value * 0.7071067811865476))
    density = jnp.exp(-0.5 * value * value) * 0.3989422804014327
    return cumul, density


BLOCK = 8
BACK = 16
ROWS = 32 * BLOCK


def k_taps(conv0, weo):
    taps = jnp.concatenate([conv0[...].astype(F32), jnp.zeros((6, 512), F32)], axis=0).astype(BF)
    weo[...] = jnp.zeros(weo.shape, BF)
    weo[pl.ds(0, 16), pl.ds(0, 512)] = taps
    weo[pl.ds(16, 16), pl.ds(512, 512)] = taps


def tables(fold, window):
    sample = lax.broadcasted_iota(jnp.int32, (256, 128), 0).astype(F32)
    lane = lax.broadcasted_iota(jnp.int32, (256, 128), 1).astype(F32)
    tens = jnp.floor((sample + 0.5) * 0.1) * 10.0
    fold[pl.ds(0, 256), :] = jnp.where(sample - tens == lane, 1.0, 0.0).astype(BF)
    tens = jnp.floor((sample - 4.5) * 0.1) * 10.0
    odd = (sample >= 5.0) & (sample - 5.0 - tens + 16.0 == lane)
    fold[pl.ds(256, 256), :] = jnp.where(odd, 1.0, 0.0).astype(BF)
    step = lax.broadcasted_iota(jnp.int32, (32, 256), 0)
    step = jnp.where(step < 16, step, step - 16) * 10
    at = lax.broadcasted_iota(jnp.int32, (32, 256), 1)
    window[:, pl.ds(0, 256)] = jnp.where((at >= step) & (at < step + 10), 1.0, 0.0)
    window[:, pl.ds(256, 256)] = jnp.where((at >= step + 5) & (at < step + 15), 1.0, 0.0)


def tall(rows):
    return jnp.concatenate([rows] * 4, axis=0)


def dot_t(left, right):
    return lax.dot_general(left, right, (((0,), (0,)), ((), ())), preferred_element_type=F32)


def dot_nt(left, right):
    return lax.dot_general(left, right, (((1,), (1,)), ((), ())), preferred_element_type=F32)


def k_forward(
    scale, pos, arrived, weo, gain, bias, weight, fgrad,
    pre1, second_count, g, gs, se, so, ne, no, istd, valid, x, he, ho, other,
    fold, window, panels, am, pre, hs,
):
    spans = panels.shape[0]
    tables(fold, window)
    arr = arrived[...].astype(F32).reshape(128, WIDE).astype(BF)
    lane = lax.broadcasted_iota(jnp.int32, (128, 128), 1).astype(F32)
    meta = arr[:, 256:384].astype(F32)
    slot = meta[:, SAMPLES - 256 : SAMPLES - 255]
    place = jnp.where(slot - 1.0 == lane, 1.0, 0.0).astype(BF)
    moved = dot_t(place, arr)[0:spans]
    late = pltpu.roll(moved, WIDE - 160, 1)
    both = jnp.concatenate([moved[:, 0:256], late[:, 0:256]], axis=1)
    panels[...] = jnp.broadcast_to(both[:, None, :], panels.shape)
    length = moved[:, SAMPLES + 1 : SAMPLES + 2] + 214.0
    count = jnp.broadcast_to(jnp.floor((length - 9.5) * 0.2) + 1.0, (spans, 128))
    valid[...] = jnp.broadcast_to(count[:, None, :], valid.shape)
    second_count[...] = jnp.floor((count - 2.5) * 0.5) + 1.0
    frame = lax.broadcasted_iota(jnp.int32, (32, 128), 0).astype(F32)

    def block(b, carry):
        base = b * BLOCK

        def patch(q, carry):
            p = base + q
            count = tall(valid[p])
            keep_e, keep_o = 2.0 * frame < count, 2.0 * frame + 1.0 < count
            rows = pl.ds(pl.multiple_of(q * 32, 32), 32)
            for t in range(4):
                early = panels[p, :, pl.ds((t % 2) * 128, 128)]
                late = panels[p, :, pl.ds(256 + (t % 2) * 128, 128)]
                part = jnp.concatenate([early, early, late, late], axis=0)
                part = jnp.where(keep_e if t < 2 else keep_o, part * window[:, pl.ds(t * 128, 128)], 0.0)
                am[rows, pl.ds(t * 128, 128)] = part.astype(BF)
            return carry

        lax.fori_loop(0, BLOCK, patch, 0, unroll=2)
        every = pl.ds(pl.multiple_of(b * ROWS, ROWS), ROWS)
        xs = jnp.dot(am[...], fold[...], preferred_element_type=F32).astype(BF)
        x[every, :] = xs
        pre[...] = jnp.dot(xs, weo[...], preferred_element_type=F32)

        def norm(q, carry):
            p = base + q
            count = valid[p]
            inverse = 1.0 / count[0:1]
            wide = tall(count)
            keep_e, keep_o = 2.0 * frame < wide, 2.0 * frame + 1.0 < wide
            rows = pl.ds(pl.multiple_of(q * 32, 32), 32)
            at = pl.ds(pl.multiple_of(p * 32, 32), 32)
            for t in range(4):
                cols = pl.ds(t * 128, 128)
                e = pre[rows, cols]
                o = pre[rows, pl.ds(512 + t * 128, 128)]
                center = jnp.sum(e + o, axis=0, keepdims=True) * inverse
                e = jnp.where(keep_e, e - center, 0.0)
                o = jnp.where(keep_o, o - center, 0.0)
                variance = jnp.sum(e * e + o * o, axis=0, keepdims=True) * inverse
                rs = lax.rsqrt(variance + 1e-05)
                istd[p, :, cols] = jnp.broadcast_to(rs, (8, 128))
                scale_row, bias_row = gain[:, cols], bias[:, cols]
                for value, keep, n_ref, s_ref, h_ref in ((e, keep_e, ne, se, he), (o, keep_o, no, so, ho)):
                    value = value * rs
                    n_ref[at, cols] = value.astype(BF)
                    value = value * scale_row + bias_row
                    cumul, density = gelu_parts(value)
                    hidden = jnp.where(keep, value * cumul, 0.0)
                    s_ref[at, cols] = jnp.where(keep, cumul + value * density, 0.0).astype(BF)
                    h_ref[at, cols] = hidden.astype(BF)
                    if h_ref is he:
                        hs[rows, cols] = pltpu.roll(hidden, 31, 0).astype(BF)
            return carry

        lax.fori_loop(0, BLOCK, norm, 0, unroll=2)
        total = (
            jnp.dot(he[every, :], weight[0], preferred_element_type=F32)
            + jnp.dot(ho[every, :], weight[1], preferred_element_type=F32)
            + jnp.dot(hs[...], weight[2], preferred_element_type=F32)
        )
        for t in range(4):
            pre1[t, every, :] = total[:, t * 128 : t * 128 + 128]

        def second(q, carry):
            p = base + q
            count = tall(jnp.floor((valid[p] - 2.5) * 0.5) + 1.0)
            keep = frame < count
            at = pl.ds(pl.multiple_of(p * 32, 32), 32)
            for t in range(4):
                cols = pl.ds(t * 128, 128)
                value = pre1[t, at, :]
                cumul, density = gelu_parts(value)
                up = fgrad[p, :, cols].astype(F32) * scale
                up = jnp.concatenate([up, jnp.zeros((1, 128), F32)], axis=0)
                grad = jnp.where(keep, up * (cumul + value * density), 0.0)
                g[at, cols] = grad.astype(BF)
                gs[at, cols] = pltpu.roll(grad, 1, 0).astype(BF)
            return carry

        lax.fori_loop(0, BLOCK, second, 0, unroll=2)
        return carry

    lax.fori_loop(0, spans // BLOCK, block, 0)
    half_of(1 - pos[2], he, ho, g, gs, other)


def half_of(half, he, ho, g, gs, out):
    @pl.when(half == 0)
    def _():
        out[pl.ds(0, 512), :] = dot_t(he[...], g[...]).astype(out.dtype)
        out[pl.ds(512, 256), :] = dot_t(ho[:, pl.ds(0, 256)], g[...]).astype(out.dtype)

    @pl.when(half == 1)
    def _():
        out[pl.ds(0, 256), :] = dot_t(ho[:, pl.ds(256, 256)], g[...]).astype(out.dtype)
        out[pl.ds(256, 512), :] = dot_t(he[...], gs[...]).astype(out.dtype)


def k_half(pos, he, ho, g, gs, before, out):
    half_of(pos[2], he, ho, g, gs, out)


def k_features(pre1, count, before, feats, token):
    token[...] = jnp.zeros(token.shape, F32)
    spans = count.shape[0]

    def frame(t, carry):
        keep = count[...] > lax.convert_element_type(t, F32)
        for c in range(4):
            cols = pl.ds(c * 128, 128)
            value = pre1[c, pl.ds(t, spans, stride=32), :]
            cumul, _ = gelu_parts(value)
            feats[t, :, cols] = jnp.where(keep, value * cumul, 0.0).astype(BF)
        return carry

    lax.fori_loop(0, feats.shape[0], frame, 0)


def k_backward(
    first, g, gs, se, so, ne, no, istd, valid, x, gain, weight, start, before, small,
    de, do, dxe, dxo, sums,
):
    blocks = dxe.shape[0] // (32 * BACK)
    sums[...] = jnp.zeros(sums.shape, F32)

    def block(b, carry):
        base = (first + b) * BACK
        every = pl.ds(pl.multiple_of((first + b) * (32 * BACK), (32 * BACK)), (32 * BACK))
        de[...] = dot_nt(g[every, :], weight[0]) + dot_nt(gs[every, :], weight[2])
        do[...] = dot_nt(g[every, :], weight[1])

        def back(q, carry):
            p = base + q
            inverse = 1.0 / valid[p, pl.ds(0, 1), :]
            rows = pl.ds(pl.multiple_of(q * 32, 32), 32)
            at = pl.ds(pl.multiple_of(p * 32, 32), 32)
            here = pl.ds(pl.multiple_of((b * BACK + q) * 32, 32), 32)
            for t in range(4):
                cols = pl.ds(t * 128, 128)
                pe = de[rows, cols] * se[at, cols].astype(F32)
                po = do[rows, cols] * so[at, cols].astype(F32)
                e, o = ne[at, cols].astype(F32), no[at, cols].astype(F32)
                plain = jnp.sum(pe + po, axis=0, keepdims=True)
                mixed = jnp.sum(pe * e + po * o, axis=0, keepdims=True)
                sums[pl.ds(0, 1), cols] += mixed
                sums[pl.ds(1, 1), cols] += plain
                lead = istd[p, pl.ds(0, 1), cols] * gain[:, cols]
                plain, mixed = plain * inverse, mixed * inverse
                dxe[here, cols] = ((pe - plain - e * mixed) * lead).astype(BF)
                dxo[here, cols] = ((po - plain - o * mixed) * lead).astype(BF)
            return carry

        lax.fori_loop(0, BACK, back, 0, unroll=2)
        return carry

    lax.fori_loop(0, blocks, block, 0)
    part = x[pl.ds(first * (32 * BACK), blocks * (32 * BACK)), :]
    small[...] = start[...] + dot_t(part, dxe[...])[0:16] + dot_t(part, dxo[...])[16:32]
    small[pl.ds(10, 2), :] += sums[pl.ds(0, 2), :]


def encode(pos, arrived, conv0_weight, norm_gain, norm_bias, conv1_weight, feature_grad, scale):
    spans = feature_grad.shape[0]
    rows = spans * 32
    (weo,) = call(k_taps, [((128, 1024), BF)], [conv0_weight])
    gain, bias = norm_gain[None], norm_bias[None]
    wide = ((rows, 512), BF)
    pre1, count, g, gs, se, so, ne, no, istd, valid, x, he, ho, other = call(
        functools.partial(k_forward, scale),
        [
            ((4, rows, 128), F32), ((spans, 128), F32), wide, wide, wide, wide, wide, wide,
            ((spans, 8, 512), F32), ((spans, 8, 128), F32), ((rows, 128), BF), wide, wide, ((768, 512), BF),
        ],
        [arrived, weo, gain, bias, conv1_weight, feature_grad],
        pos,
        scratch=[
            ((512, 128), BF), ((32, 512), F32), ((spans, 8, 512), F32), ((ROWS, 512), BF), ((ROWS, 1024), F32),
            ((ROWS, 512), BF),
        ],
    )

    def features(before):
        frames = feature_grad.shape[1]
        return call(
            k_features, [((frames, spans, 512), BF), ((8, 128), F32)], [pre1, count], after=[before]
        )

    def mine(before):
        return call(k_half, [((768, 512), F32)], [he, ho, g, gs], pos, after=[before])[0]

    def backward(first, blocks, small, before):
        part, step = (32 * BACK * blocks, 512), (32 * BACK, 512)
        return call(
            functools.partial(k_backward, first),
            [((16, 512), F32)],
            [g, gs, se, so, ne, no, istd, valid, x, gain, conv1_weight, small],
            scratch=[(step, F32), (step, F32), (part, BF), (part, BF), ((8, 512), F32)],
            after=[before],
        )[0]

    return features, other, mine, backward


def body(waveform, lengths, target, conv0_weight, norm_gain, norm_bias, conv1_weight, feature_grad):
    spans = waveform.shape[1]
    devices = lax.axis_size("dp")
    frames = feature_grad.shape[2]
    pos = where_am_i()
    (packed,) = call(
        k_pack,
        [((devices, 2, WIDE), BF)],
        [],
        scratch=[
            ((spans, WIDE), F32), (waveform.shape[1:], BF), (lengths.shape, jnp.int32), (target.shape, jnp.int32),
            pltpu.SemaphoreType.DMA((3,)),
        ],
        after=[waveform[0], lengths, target],
        late=HBM,
        limit=60,
    )
    arrived = lax.all_to_all(packed, "dp", split_axis=0, concat_axis=0, tiled=True)
    scale = 1.0 / float(lax.axis_size("rep") * devices * spans * frames) ** 0.5
    features, other, mine, backward = encode(
        pos, arrived, conv0_weight, norm_gain, norm_bias, conv1_weight, feature_grad[0], scale
    )
    full, conv0, gain, bias, feats = reduce_all(pos, other, mine, backward, features)
    return (feats[None], conv0, gain, bias, full.reshape(conv1_weight.shape))


def solution(mesh):
    placed = (
        P("rep", "dp", None),
        P("rep", "dp"),
        P("rep", "dp"),
        P(),
        P(),
        P(),
        P(),
        P("rep", "dp", None, None),
    )
    return jax.shard_map(
        body,
        mesh=mesh,
        in_specs=placed,
        out_specs=(P("rep", "dp", None, None), P(), P(), P(), P()),
        check_vma=False,
    )
```

```python
import functools

import jax
import jax.numpy as jnp
from jax import lax
from jax.experimental import pallas as pl
from jax.experimental.pallas import tpu as pltpu
from jax.sharding import PartitionSpec as P

BF, F32 = jnp.bfloat16, jnp.float32
VM = pl.BlockSpec(memory_space=pltpu.VMEM)
SM = pl.BlockSpec(memory_space=pltpu.SMEM)
ANY = pl.BlockSpec(memory_space=pl.ANY)
HBM = pl.BlockSpec(memory_space=pltpu.HBM)
BOTH = ("dp", "rep")
SAMPLES = 320


def call(kernel, outs, ins, scal=None, scratch=(), after=(), late=ANY, limit=20):
    specs = [VM] * len(ins) + [late] * len(after)
    ins = [*ins, *after]
    if scal is not None:
        specs = [SM] + specs
        ins = [scal, *ins]
    shapes = [jax.ShapeDtypeStruct(s, d) for s, d in outs]
    return pl.pallas_call(
        kernel,
        out_shape=shapes,
        in_specs=specs,
        out_specs=[VM] * len(outs),
        scratch_shapes=[pltpu.VMEM(*s) if isinstance(s, tuple) else s for s in scratch],
        compiler_params=pltpu.CompilerParams(vmem_limit_bytes=limit << 20),
    )(*ins)


def perms():
    every = [(z, y, c, x) for z in range(8) for y in range(4) for c in range(2) for x in range(4)]

    def lin(z, y, c, x):
        return ((z * 4 + y) * 2 + c) * 4 + x

    def build(move):
        return [(lin(*p), lin(*move(*p))) for p in every]

    def along(first, k):
        def move(z, y, c, x):
            if (c == 1) == first:
                return (z, y, c, (x + k) % 4)
            return (z, (y + k) % 4, c, x)

        return build(move)

    core = build(lambda z, y, c, x: (z, y, 1 - c, x))
    one = [along(True, k) for k in range(1, 4)]
    two = [along(False, k) for k in range(1, 4)]
    steps = [build(lambda z, y, c, x, flip=flip: (z ^ flip, y, c, x)) for flip in (1, 3, 7)]
    return core, one, two, steps


def send(value, perm):
    return lax.ppermute(value, BOTH, perm)


def k_scatter_one(pos, own, got, m1, m2, m3, keep):
    a1 = pos[0]
    for k, out in ((0, None), (1, m1), (2, m2), (3, m3)):
        j = (a1 + k) & 3
        rows = pl.ds(pl.multiple_of(j * 192, 192), 192)
        total = own[rows, :] + got[rows, :].astype(F32)
        if out is None:
            keep[...] = total
        else:
            out[...] = total.astype(BF)


def k_scatter_two(pos, keep, r1, r2, r3, before, m1, m2, m3, keep2):
    a2 = pos[1]
    for k, out in ((0, None), (1, m1), (2, m2), (3, m3)):
        rows = pl.ds(pl.multiple_of(((a2 + k) & 3) * 48, 16), 48)
        total = keep[rows, :] + r1[rows, :].astype(F32) + r2[rows, :].astype(F32) + r3[rows, :].astype(F32)
        if out is None:
            keep2[...] = total
        else:
            out[...] = total.astype(BF)


def lift(ref, at):
    return ref[pl.ds(at, 16), :].astype(F32) + ref[pl.ds(at + 16, 16), :].astype(F32)


def put(out, at, value):
    high = value.astype(BF)
    out[pl.ds(at, 16), :] = high
    out[pl.ds(at + 16, 16), :] = (value - high.astype(F32)).astype(BF)


def k_sum_two(keep2, r1, r2, r3, small, out):
    out[pl.ds(0, 48), :] = (
        (keep2[...] + r2[...].astype(F32)) + (r1[...].astype(F32) + r3[...].astype(F32))
    ).astype(BF)
    put(out, 48, small[...])


def k_pair(a, b, *rest):
    out = rest[-1]
    head = pl.ds(0, 48)
    out[head, :] = (a[head, :].astype(F32) + b[head, :].astype(F32)).astype(BF)
    put(out, 48, lift(a, 48) + lift(b, 48))


def k_join_two(own, r1, r2, r3, out):
    for k, part in enumerate((own, r1, r2, r3)):
        out[pl.ds(48 * k, 48), :] = part[pl.ds(0, 48), :]
    put(out, 192, (lift(own, 48) + lift(r2, 48)) + (lift(r1, 48) + lift(r3, 48)))


def k_join_one(own, r1, r2, r3, out):
    for k, part in enumerate((own, r1, r2, r3)):
        out[pl.ds(192 * k, 192), :] = part[pl.ds(0, 192), :]
    put(out, 768, (lift(own, 192) + lift(r2, 192)) + (lift(r1, 192) + lift(r3, 192)))


def order(ref, out, j1, first, second):
    for j2 in range(4):
        at = ((first - j1) & 3) * 4 + ((second - j2) & 3)
        out[pl.ds((j1 * 4 + j2) * 48, 48), :] = ref[pl.ds(pl.multiple_of(at * 48, 16), 48), :].astype(F32)


def flush(core, out, rest, sems, ref, first, second):
    copies = []
    for j1 in range(4):
        order(ref, rest, j1, first, second)
        at = pl.multiple_of(core * 768 + j1 * 192, 192)
        copy = pltpu.make_async_copy(rest.at[pl.ds(j1 * 192, 192), :], out.at[pl.ds(at, 192), :], sems.at[j1])
        copy.start()
        copies.append(copy)
    return copies


def k_early(pos, own, full, rest, sems):
    for copy in flush(pos[2], full, rest, sems, own, pos[0], pos[1]):
        copy.wait()


def k_final(pos, own, got, half, full, conv0, gain, bias, rest, sems, conv0_row, gain_row, bias_row, small_sems):
    total = lift(own, 768) + lift(got, 768)
    conv0_row[...] = total[0:10]
    gain_row[...] = total[10:11]
    bias_row[...] = total[11:12]
    copies = [
        pltpu.make_async_copy(source, out, small_sems.at[n])
        for n, (source, out) in enumerate(((conv0_row, conv0), (gain_row, gain), (bias_row, bias)))
    ]
    for copy in copies:
        copy.start()
    copies += flush(1 - pos[2], full, rest, sems, got, pos[1], pos[0])
    for copy in copies:
        copy.wait()


def where_am_i():
    dp, x = lax.axis_index("dp"), lax.axis_index("rep")
    core, y = lax.rem(dp, 2), lax.rem(lax.div(dp, 2), 4)
    first = jnp.where(core == 0, y, x)
    second = jnp.where(core == 0, x, y)
    return jnp.stack([first, second, core]).astype(jnp.int32)


def reduce_all(pos, other, mine, backward, features):
    core, one, two, steps = perms()
    row = 512
    third = ((48, row), BF)
    got = send(other, core)
    own = mine(other)
    m1, m2, m3, keep = call(k_scatter_one, [((192, row), BF)] * 3 + [((192, row), F32)], [own, got], pos)
    r = [send(m, p) for m, p in zip((m1, m2, m3), one)]
    small = backward(0, 2, jnp.zeros((16, row), F32), keep)
    m1, m2, m3, keep2 = call(
        k_scatter_two, [third] * 3 + [((48, row), F32)], [keep, *r], pos, after=[small]
    )
    r = [send(m, p) for m, p in zip((m1, m2, m3), two)]
    small = backward(2, 1, small, keep2)
    (a,) = call(k_sum_two, [((80, row), BF)], [keep2, *r, small])
    feats = None
    for n, step in enumerate(steps):
        b = send(a, step)
        if n == 1:
            feats, token = features(a)
        (a,) = call(k_pair, [((80, row), BF)], [a, b], after=[token] if n == 1 else [])
    r = [send(a, p) for p in two]
    (a,) = call(k_join_two, [((224, row), BF)], [a, *r])
    r = [send(a, p) for p in one]
    (a,) = call(k_join_one, [((800, row), BF)], [a, *r])
    got = send(a, core)
    room = [pltpu.VMEM((768, row), F32), pltpu.SemaphoreType.DMA((4,))]
    grant = pltpu.CompilerParams(vmem_limit_bytes=20 << 20)
    whole = jax.ShapeDtypeStruct((1536, row), F32)
    half = pl.pallas_call(
        k_early, out_shape=whole, in_specs=[SM, VM], out_specs=ANY, scratch_shapes=room, compiler_params=grant
    )(pos, a)
    full, conv0, gain, bias = pl.pallas_call(
        k_final,
        out_shape=[whole] + [jax.ShapeDtypeStruct((n, row), F32) for n in (10, 1, 1)],
        in_specs=[SM, VM, VM, ANY],
        out_specs=[ANY] * 4,
        scratch_shapes=[*room, *(pltpu.VMEM((n, row), F32) for n in (10, 1, 1)), pltpu.SemaphoreType.DMA((3,))],
        input_output_aliases={3: 0},
        compiler_params=grant,
    )(pos, a, got, half)
    return full, conv0, gain[0], bias[0], jnp.transpose(feats, (1, 0, 2))


WIDE = 384


def k_pack(wave_in, length_in, target_in, out, rows, wave, length, target, sems):
    copies = [
        pltpu.make_async_copy(source, place, sems.at[n])
        for n, (source, place) in enumerate(((wave_in, wave), (length_in, length), (target_in, target)))
    ]
    for copy in copies:
        copy.start()
    for copy in copies:
        copy.wait()
    spans = wave.shape[0]
    goal = target[...].astype(F32)
    device = jnp.floor((goal + 0.5) * (1.0 / spans))
    slot = goal - device * spans
    up = lax.broadcasted_iota(jnp.int32, (spans, spans), 0)
    across = lax.broadcasted_iota(jnp.int32, (spans, spans), 1)

    def column(row):
        return jnp.sum(jnp.where(up == across, jnp.broadcast_to(row, (spans, spans)), 0.0), axis=1, keepdims=True)

    same = (column(device) == device) & (up < across)
    rank = jnp.sum(jnp.where(same, 1.0, 0.0), axis=0, keepdims=True)
    bucket = (device * 2.0 + rank).astype(jnp.int32)
    places = out.shape[0] * out.shape[1]
    pick = lax.broadcasted_iota(jnp.int32, (places, spans), 0) == bucket
    pick = jnp.where(pick, 1.0, 0.0).astype(BF)
    rows[...] = jnp.zeros(rows.shape, F32)
    rows[:, pl.ds(0, SAMPLES)] = wave[...].astype(F32)
    lane = lax.broadcasted_iota(jnp.int32, (spans, 128), 1)
    tail = rows[:, pl.ds(256, 128)]
    tail = jnp.where(lane == SAMPLES - 256, column(slot) + 1.0, tail)
    tail = jnp.where(lane == SAMPLES - 255, column(length[...].astype(F32)) - 214.0, tail)
    rows[:, pl.ds(256, 128)] = tail
    packed = jnp.dot(pick, rows[...].astype(BF), preferred_element_type=F32)
    out[...] = packed.reshape(out.shape).astype(BF)


def gelu_parts(value):
    cumul = 0.5 * (1.0 + lax.erf(value * 0.7071067811865476))
    density = jnp.exp(-0.5 * value * value) * 0.3989422804014327
    return cumul, density


BLOCK = 16
BACK = 16
ROWS = 32 * BLOCK


def k_taps(conv0, weo):
    taps = jnp.concatenate([conv0[...].astype(F32), jnp.zeros((6, 512), F32)], axis=0).astype(BF)
    weo[...] = jnp.zeros(weo.shape, BF)
    weo[pl.ds(0, 16), pl.ds(0, 512)] = taps
    weo[pl.ds(16, 16), pl.ds(512, 512)] = taps


def tables(fold, window):
    sample = lax.broadcasted_iota(jnp.int32, (256, 128), 0).astype(F32)
    lane = lax.broadcasted_iota(jnp.int32, (256, 128), 1).astype(F32)
    tens = jnp.floor((sample + 0.5) * 0.1) * 10.0
    fold[pl.ds(0, 256), :] = jnp.where(sample - tens == lane, 1.0, 0.0).astype(BF)
    tens = jnp.floor((sample - 4.5) * 0.1) * 10.0
    odd = (sample >= 5.0) & (sample - 5.0 - tens + 16.0 == lane)
    fold[pl.ds(256, 256), :] = jnp.where(odd, 1.0, 0.0).astype(BF)
    step = lax.broadcasted_iota(jnp.int32, (32, 256), 0)
    step = jnp.where(step < 16, step, step - 16) * 10
    at = lax.broadcasted_iota(jnp.int32, (32, 256), 1)
    window[:, pl.ds(0, 256)] = jnp.where((at >= step) & (at < step + 10), 1.0, 0.0)
    window[:, pl.ds(256, 256)] = jnp.where((at >= step + 5) & (at < step + 15), 1.0, 0.0)


def tall(rows):
    return jnp.concatenate([rows] * 4, axis=0)


def dot_t(left, right):
    return lax.dot_general(left, right, (((0,), (0,)), ((), ())), preferred_element_type=F32)


def dot_nt(left, right):
    return lax.dot_general(left, right, (((1,), (1,)), ((), ())), preferred_element_type=F32)


def k_forward(
    scale, pos, arrived, weo, gain, bias, weight, fgrad,
    pre1, second_count, g, gs, se, so, ne, no, istd, valid, x, he, ho, other,
    fold, window, panels, am, pre, hs,
):
    spans = panels.shape[0]
    tables(fold, window)
    arr = arrived[...].astype(F32).reshape(128, WIDE).astype(BF)
    lane = lax.broadcasted_iota(jnp.int32, (128, 128), 1).astype(F32)
    meta = arr[:, 256:384].astype(F32)
    slot = meta[:, SAMPLES - 256 : SAMPLES - 255]
    place = jnp.where(slot - 1.0 == lane, 1.0, 0.0).astype(BF)
    moved = dot_t(place, arr)[0:spans]
    late = pltpu.roll(moved, WIDE - 160, 1)
    both = jnp.concatenate([moved[:, 0:256], late[:, 0:256]], axis=1)
    panels[...] = jnp.broadcast_to(both[:, None, :], panels.shape)
    length = moved[:, SAMPLES + 1 : SAMPLES + 2] + 214.0
    count = jnp.broadcast_to(jnp.floor((length - 9.5) * 0.2) + 1.0, (spans, 128))
    valid[...] = jnp.broadcast_to(count[:, None, :], valid.shape)
    second_count[...] = jnp.floor((count - 2.5) * 0.5) + 1.0
    frame = lax.broadcasted_iota(jnp.int32, (32, 128), 0).astype(F32)

    def block(b, carry):
        base = b * BLOCK

        def patch(q, carry):
            p = base + q
            count = tall(valid[p])
            keep_e, keep_o = 2.0 * frame < count, 2.0 * frame + 1.0 < count
            rows = pl.ds(pl.multiple_of(q * 32, 32), 32)
            for t in range(4):
                early = panels[p, :, pl.ds((t % 2) * 128, 128)]
                late = panels[p, :, pl.ds(256 + (t % 2) * 128, 128)]
                part = jnp.concatenate([early, early, late, late], axis=0)
                part = jnp.where(keep_e if t < 2 else keep_o, part * window[:, pl.ds(t * 128, 128)], 0.0)
                am[rows, pl.ds(t * 128, 128)] = part.astype(BF)
            return carry

        lax.fori_loop(0, BLOCK, patch, 0, unroll=BLOCK)
        every = pl.ds(pl.multiple_of(b * ROWS, ROWS), ROWS)
        xs = jnp.dot(am[...], fold[...], preferred_element_type=F32).astype(BF)
        x[every, :] = xs
        pre[...] = jnp.dot(xs, weo[...], preferred_element_type=F32)

        def norm(q, carry):
            p = base + q
            count = valid[p]
            inverse = 1.0 / count[0:1]
            wide = tall(count)
            keep_e, keep_o = 2.0 * frame < wide, 2.0 * frame + 1.0 < wide
            rows = pl.ds(pl.multiple_of(q * 32, 32), 32)
            at = pl.ds(pl.multiple_of(p * 32, 32), 32)
            for t in range(4):
                cols = pl.ds(t * 128, 128)
                e = pre[rows, cols]
                o = pre[rows, pl.ds(512 + t * 128, 128)]
                center = jnp.sum(e + o, axis=0, keepdims=True) * inverse
                e = jnp.where(keep_e, e - center, 0.0)
                o = jnp.where(keep_o, o - center, 0.0)
                variance = jnp.sum(e * e + o * o, axis=0, keepdims=True) * inverse
                rs = lax.rsqrt(variance + 1e-05)
                istd[p, :, cols] = jnp.broadcast_to(rs, (8, 128))
                scale_row, bias_row = gain[:, cols], bias[:, cols]
                for value, keep, n_ref, s_ref, h_ref in ((e, keep_e, ne, se, he), (o, keep_o, no, so, ho)):
                    value = value * rs
                    n_ref[at, cols] = value.astype(BF)
                    value = value * scale_row + bias_row
                    cumul, density = gelu_parts(value)
                    hidden = jnp.where(keep, value * cumul, 0.0)
                    s_ref[at, cols] = jnp.where(keep, cumul + value * density, 0.0).astype(BF)
                    h_ref[at, cols] = hidden.astype(BF)
                    if h_ref is he:
                        hs[rows, cols] = pltpu.roll(hidden, 31, 0).astype(BF)
            return carry

        lax.fori_loop(0, BLOCK, norm, 0, unroll=2)
        total = (
            jnp.dot(he[every, :], weight[0], preferred_element_type=F32)
            + jnp.dot(ho[every, :], weight[1], preferred_element_type=F32)
            + jnp.dot(hs[...], weight[2], preferred_element_type=F32)
        )
        for t in range(4):
            pre1[t, every, :] = total[:, t * 128 : t * 128 + 128]

        def second(q, carry):
            p = base + q
            count = tall(jnp.floor((valid[p] - 2.5) * 0.5) + 1.0)
            keep = frame < count
            at = pl.ds(pl.multiple_of(p * 32, 32), 32)
            for t in range(4):
                cols = pl.ds(t * 128, 128)
                value = pre1[t, at, :]
                cumul, density = gelu_parts(value)
                up = fgrad[p, :, cols].astype(F32) * scale
                up = jnp.concatenate([up, jnp.zeros((1, 128), F32)], axis=0)
                grad = jnp.where(keep, up * (cumul + value * density), 0.0)
                g[at, cols] = grad.astype(BF)
                gs[at, cols] = pltpu.roll(grad, 1, 0).astype(BF)
            return carry

        lax.fori_loop(0, BLOCK, second, 0, unroll=BLOCK)
        return carry

    lax.fori_loop(0, spans // BLOCK, block, 0)
    half_of(1 - pos[2], he, ho, g, gs, other)


def half_of(half, he, ho, g, gs, out):
    @pl.when(half == 0)
    def _():
        out[pl.ds(0, 512), :] = dot_t(he[...], g[...]).astype(out.dtype)
        out[pl.ds(512, 256), :] = dot_t(ho[:, pl.ds(0, 256)], g[...]).astype(out.dtype)

    @pl.when(half == 1)
    def _():
        out[pl.ds(0, 256), :] = dot_t(ho[:, pl.ds(256, 256)], g[...]).astype(out.dtype)
        out[pl.ds(256, 512), :] = dot_t(he[...], gs[...]).astype(out.dtype)


def k_half(pos, he, ho, g, gs, before, out):
    half_of(pos[2], he, ho, g, gs, out)


def k_features(pre1, count, before, feats, token):
    token[...] = jnp.zeros(token.shape, F32)
    spans = count.shape[0]

    def frame(t, carry):
        keep = count[...] > lax.convert_element_type(t, F32)
        for c in range(4):
            cols = pl.ds(c * 128, 128)
            value = pre1[c, pl.ds(t, spans, stride=32), :]
            cumul, _ = gelu_parts(value)
            feats[t, :, cols] = jnp.where(keep, value * cumul, 0.0).astype(BF)
        return carry

    lax.fori_loop(0, feats.shape[0], frame, 0, unroll=True)


def k_backward(
    first, g, gs, se, so, ne, no, istd, valid, x, gain, weight, start, before, small,
    de, do, dxe, dxo, sums,
):
    blocks = dxe.shape[0] // (32 * BACK)
    sums[...] = jnp.zeros(sums.shape, F32)

    def block(b, carry):
        base = (first + b) * BACK
        every = pl.ds(pl.multiple_of((first + b) * (32 * BACK), (32 * BACK)), (32 * BACK))
        de[...] = dot_nt(g[every, :], weight[0]) + dot_nt(gs[every, :], weight[2])
        do[...] = dot_nt(g[every, :], weight[1])

        def back(q, carry):
            p = base + q
            inverse = 1.0 / valid[p, pl.ds(0, 1), :]
            rows = pl.ds(pl.multiple_of(q * 32, 32), 32)
            at = pl.ds(pl.multiple_of(p * 32, 32), 32)
            here = pl.ds(pl.multiple_of((b * BACK + q) * 32, 32), 32)
            for t in range(4):
                cols = pl.ds(t * 128, 128)
                pe = de[rows, cols] * se[at, cols].astype(F32)
                po = do[rows, cols] * so[at, cols].astype(F32)
                e, o = ne[at, cols].astype(F32), no[at, cols].astype(F32)
                plain = jnp.sum(pe + po, axis=0, keepdims=True)
                mixed = jnp.sum(pe * e + po * o, axis=0, keepdims=True)
                sums[pl.ds(0, 1), cols] += mixed
                sums[pl.ds(1, 1), cols] += plain
                lead = istd[p, pl.ds(0, 1), cols] * gain[:, cols]
                plain, mixed = plain * inverse, mixed * inverse
                dxe[here, cols] = ((pe - plain - e * mixed) * lead).astype(BF)
                dxo[here, cols] = ((po - plain - o * mixed) * lead).astype(BF)
            return carry

        lax.fori_loop(0, BACK, back, 0, unroll=BACK)
        return carry

    lax.fori_loop(0, blocks, block, 0)
    part = x[pl.ds(first * (32 * BACK), blocks * (32 * BACK)), :]
    small[...] = start[...] + dot_t(part, dxe[...])[0:16] + dot_t(part, dxo[...])[16:32]
    small[pl.ds(10, 2), :] += sums[pl.ds(0, 2), :]


def encode(pos, arrived, conv0_weight, norm_gain, norm_bias, conv1_weight, feature_grad, scale):
    spans = feature_grad.shape[0]
    rows = spans * 32
    (weo,) = call(k_taps, [((128, 1024), BF)], [conv0_weight])
    gain, bias = norm_gain[None], norm_bias[None]
    wide = ((rows, 512), BF)
    pre1, count, g, gs, se, so, ne, no, istd, valid, x, he, ho, other = call(
        functools.partial(k_forward, scale),
        [
            ((4, rows, 128), F32), ((spans, 128), F32), wide, wide, wide, wide, wide, wide,
            ((spans, 8, 512), F32), ((spans, 8, 128), F32), ((rows, 128), BF), wide, wide, ((768, 512), BF),
        ],
        [arrived, weo, gain, bias, conv1_weight, feature_grad],
        pos,
        scratch=[
            ((512, 128), BF), ((32, 512), F32), ((spans, 8, 512), F32), ((ROWS, 512), BF), ((ROWS, 1024), F32),
            ((ROWS, 512), BF),
        ],
    )

    def features(before):
        frames = feature_grad.shape[1]
        return call(
            k_features, [((frames, spans, 512), BF), ((8, 128), F32)], [pre1, count], after=[before]
        )

    def mine(before):
        return call(k_half, [((768, 512), F32)], [he, ho, g, gs], pos, after=[before])[0]

    def backward(first, blocks, small, before):
        part, step = (32 * BACK * blocks, 512), (32 * BACK, 512)
        return call(
            functools.partial(k_backward, first),
            [((16, 512), F32)],
            [g, gs, se, so, ne, no, istd, valid, x, gain, conv1_weight, small],
            scratch=[(step, F32), (step, F32), (part, BF), (part, BF), ((8, 512), F32)],
            after=[before],
        )[0]

    return features, other, mine, backward


def body(waveform, lengths, target, conv0_weight, norm_gain, norm_bias, conv1_weight, feature_grad):
    spans = waveform.shape[1]
    devices = lax.axis_size("dp")
    frames = feature_grad.shape[2]
    pos = where_am_i()
    (packed,) = call(
        k_pack,
        [((devices, 2, WIDE), BF)],
        [],
        scratch=[
            ((spans, WIDE), F32), (waveform.shape[1:], BF), (lengths.shape, jnp.int32), (target.shape, jnp.int32),
            pltpu.SemaphoreType.DMA((3,)),
        ],
        after=[waveform[0], lengths, target],
        late=HBM,
        limit=60,
    )
    arrived = lax.all_to_all(packed, "dp", split_axis=0, concat_axis=0, tiled=True)
    scale = 1.0 / float(lax.axis_size("rep") * devices * spans * frames) ** 0.5
    features, other, mine, backward = encode(
        pos, arrived, conv0_weight, norm_gain, norm_bias, conv1_weight, feature_grad[0], scale
    )
    full, conv0, gain, bias, feats = reduce_all(pos, other, mine, backward, features)
    return (feats[None], conv0, gain, bias, full.reshape(conv1_weight.shape))


def solution(mesh):
    placed = (
        P("rep", "dp", None),
        P("rep", "dp"),
        P("rep", "dp"),
        P(),
        P(),
        P(),
        P(),
        P("rep", "dp", None, None),
    )
    return jax.shard_map(
        body,
        mesh=mesh,
        in_specs=placed,
        out_specs=(P("rep", "dp", None, None), P(), P(), P(), P()),
        check_vma=False,
    )
```

```python
import functools

import jax
import jax.numpy as jnp
from jax import lax
from jax.experimental import pallas as pl
from jax.experimental.pallas import tpu as pltpu
from jax.sharding import PartitionSpec as P

BF, F32 = jnp.bfloat16, jnp.float32
VM = pl.BlockSpec(memory_space=pltpu.VMEM)
SM = pl.BlockSpec(memory_space=pltpu.SMEM)
ANY = pl.BlockSpec(memory_space=pl.ANY)
HBM = pl.BlockSpec(memory_space=pltpu.HBM)
BOTH = ("dp", "rep")
SAMPLES = 320


def call(kernel, outs, ins, scal=None, scratch=(), after=(), late=ANY, limit=20):
    specs = [VM] * len(ins) + [late] * len(after)
    ins = [*ins, *after]
    if scal is not None:
        specs = [SM] + specs
        ins = [scal, *ins]
    shapes = [jax.ShapeDtypeStruct(s, d) for s, d in outs]
    return pl.pallas_call(
        kernel,
        out_shape=shapes,
        in_specs=specs,
        out_specs=[VM] * len(outs),
        scratch_shapes=[pltpu.VMEM(*s) if isinstance(s, tuple) else s for s in scratch],
        compiler_params=pltpu.CompilerParams(vmem_limit_bytes=limit << 20),
    )(*ins)


def perms():
    every = [(z, y, c, x) for z in range(8) for y in range(4) for c in range(2) for x in range(4)]

    def lin(z, y, c, x):
        return ((z * 4 + y) * 2 + c) * 4 + x

    def build(move):
        return [(lin(*p), lin(*move(*p))) for p in every]

    def along(first, k):
        def move(z, y, c, x):
            if (c == 1) == first:
                return (z, y, c, (x + k) % 4)
            return (z, (y + k) % 4, c, x)

        return build(move)

    core = build(lambda z, y, c, x: (z, y, 1 - c, x))
    one = [along(True, k) for k in range(1, 4)]
    two = [along(False, k) for k in range(1, 4)]
    steps = [build(lambda z, y, c, x, flip=flip: (z ^ flip, y, c, x)) for flip in (1, 3, 7)]
    return core, one, two, steps


def send(value, perm):
    return lax.ppermute(value, BOTH, perm)


def k_scatter_one(pos, own, got, m1, m2, m3, keep):
    a1 = pos[0]
    for k, out in ((0, None), (1, m1), (2, m2), (3, m3)):
        j = (a1 + k) & 3
        rows = pl.ds(pl.multiple_of(j * 192, 192), 192)
        total = own[rows, :] + got[rows, :].astype(F32)
        if out is None:
            keep[...] = total
        else:
            out[...] = total.astype(BF)


def k_scatter_two(pos, keep, r1, r2, r3, before, m1, m2, m3, keep2):
    a2 = pos[1]
    for k, out in ((0, None), (1, m1), (2, m2), (3, m3)):
        rows = pl.ds(pl.multiple_of(((a2 + k) & 3) * 48, 16), 48)
        total = keep[rows, :] + r1[rows, :].astype(F32) + r2[rows, :].astype(F32) + r3[rows, :].astype(F32)
        if out is None:
            keep2[...] = total
        else:
            out[...] = total.astype(BF)


def lift(ref, at):
    return ref[pl.ds(at, 16), :].astype(F32) + ref[pl.ds(at + 16, 16), :].astype(F32)


def put(out, at, value):
    high = value.astype(BF)
    out[pl.ds(at, 16), :] = high
    out[pl.ds(at + 16, 16), :] = (value - high.astype(F32)).astype(BF)


def k_sum_two(keep2, r1, r2, r3, small, out):
    out[pl.ds(0, 48), :] = (
        (keep2[...] + r2[...].astype(F32)) + (r1[...].astype(F32) + r3[...].astype(F32))
    ).astype(BF)
    put(out, 48, small[...])


def k_pair(a, b, *rest):
    out = rest[-1]
    head = pl.ds(0, 48)
    out[head, :] = (a[head, :].astype(F32) + b[head, :].astype(F32)).astype(BF)
    put(out, 48, lift(a, 48) + lift(b, 48))


def k_join_two(own, r1, r2, r3, out):
    for k, part in enumerate((own, r1, r2, r3)):
        out[pl.ds(48 * k, 48), :] = part[pl.ds(0, 48), :]
    put(out, 192, (lift(own, 48) + lift(r2, 48)) + (lift(r1, 48) + lift(r3, 48)))


def k_join_one(own, r1, r2, r3, out):
    for k, part in enumerate((own, r1, r2, r3)):
        out[pl.ds(192 * k, 192), :] = part[pl.ds(0, 192), :]
    put(out, 768, (lift(own, 192) + lift(r2, 192)) + (lift(r1, 192) + lift(r3, 192)))


def order(ref, out, j1, first, second):
    for j2 in range(4):
        at = ((first - j1) & 3) * 4 + ((second - j2) & 3)
        out[pl.ds((j1 * 4 + j2) * 48, 48), :] = ref[pl.ds(pl.multiple_of(at * 48, 16), 48), :].astype(F32)


def flush(core, out, rest, sems, ref, first, second):
    copies = []
    for j1 in range(4):
        order(ref, rest, j1, first, second)
        at = pl.multiple_of(core * 768 + j1 * 192, 192)
        copy = pltpu.make_async_copy(rest.at[pl.ds(j1 * 192, 192), :], out.at[pl.ds(at, 192), :], sems.at[j1])
        copy.start()
        copies.append(copy)
    return copies


def k_early(pos, own, full, rest, sems):
    for copy in flush(pos[2], full, rest, sems, own, pos[0], pos[1]):
        copy.wait()


def k_final(pos, own, got, half, full, conv0, gain, bias, rest, sems, conv0_row, gain_row, bias_row, small_sems):
    total = lift(own, 768) + lift(got, 768)
    conv0_row[...] = total[0:10]
    gain_row[...] = total[10:11]
    bias_row[...] = total[11:12]
    copies = [
        pltpu.make_async_copy(source, out, small_sems.at[n])
        for n, (source, out) in enumerate(((conv0_row, conv0), (gain_row, gain), (bias_row, bias)))
    ]
    for copy in copies:
        copy.start()
    copies += flush(1 - pos[2], full, rest, sems, got, pos[1], pos[0])
    for copy in copies:
        copy.wait()


def where_am_i():
    dp, x = lax.axis_index("dp"), lax.axis_index("rep")
    core, y = lax.rem(dp, 2), lax.rem(lax.div(dp, 2), 4)
    first = jnp.where(core == 0, y, x)
    second = jnp.where(core == 0, x, y)
    return jnp.stack([first, second, core]).astype(jnp.int32)


def reduce_all(pos, other, mine, backward, features):
    core, one, two, steps = perms()
    row = 512
    third = ((48, row), BF)
    got = send(other, core)
    own = mine(other)
    m1, m2, m3, keep = call(k_scatter_one, [((192, row), BF)] * 3 + [((192, row), F32)], [own, got], pos)
    r = [send(m, p) for m, p in zip((m1, m2, m3), one)]
    small = backward(0, 2, jnp.zeros((16, row), F32), keep)
    m1, m2, m3, keep2 = call(
        k_scatter_two, [third] * 3 + [((48, row), F32)], [keep, *r], pos, after=[small]
    )
    r = [send(m, p) for m, p in zip((m1, m2, m3), two)]
    small = backward(2, 1, small, keep2)
    (a,) = call(k_sum_two, [((80, row), BF)], [keep2, *r, small])
    feats = None
    for n, step in enumerate(steps):
        b = send(a, step)
        if n == 1:
            feats, token = features(a)
        (a,) = call(k_pair, [((80, row), BF)], [a, b], after=[token] if n == 1 else [])
    r = [send(a, p) for p in two]
    (a,) = call(k_join_two, [((224, row), BF)], [a, *r])
    r = [send(a, p) for p in one]
    (a,) = call(k_join_one, [((800, row), BF)], [a, *r])
    got = send(a, core)
    room = [pltpu.VMEM((768, row), F32), pltpu.SemaphoreType.DMA((4,))]
    grant = pltpu.CompilerParams(vmem_limit_bytes=20 << 20)
    whole = jax.ShapeDtypeStruct((1536, row), F32)
    half = pl.pallas_call(
        k_early, out_shape=whole, in_specs=[SM, VM], out_specs=ANY, scratch_shapes=room, compiler_params=grant
    )(pos, a)
    full, conv0, gain, bias = pl.pallas_call(
        k_final,
        out_shape=[whole] + [jax.ShapeDtypeStruct((n, row), F32) for n in (10, 1, 1)],
        in_specs=[SM, VM, VM, ANY],
        out_specs=[ANY] * 4,
        scratch_shapes=[*room, *(pltpu.VMEM((n, row), F32) for n in (10, 1, 1)), pltpu.SemaphoreType.DMA((3,))],
        input_output_aliases={3: 0},
        compiler_params=grant,
    )(pos, a, got, half)
    return full, conv0, gain[0], bias[0], jnp.transpose(feats, (1, 0, 2))


WIDE = 384


def k_pack(wave_in, length_in, target_in, out, rows, wave, length, target, sems):
    copies = [
        pltpu.make_async_copy(source, place, sems.at[n])
        for n, (source, place) in enumerate(((wave_in, wave), (length_in, length), (target_in, target)))
    ]
    for copy in copies:
        copy.start()
    for copy in copies:
        copy.wait()
    spans = wave.shape[0]
    goal = target[...].astype(F32)
    device = jnp.floor((goal + 0.5) * (1.0 / spans))
    slot = goal - device * spans
    up = lax.broadcasted_iota(jnp.int32, (spans, spans), 0)
    across = lax.broadcasted_iota(jnp.int32, (spans, spans), 1)

    def column(row):
        return jnp.sum(jnp.where(up == across, jnp.broadcast_to(row, (spans, spans)), 0.0), axis=1, keepdims=True)

    same = (column(device) == device) & (up < across)
    rank = jnp.sum(jnp.where(same, 1.0, 0.0), axis=0, keepdims=True)
    bucket = (device * 2.0 + rank).astype(jnp.int32)
    places = out.shape[0] * out.shape[1]
    pick = lax.broadcasted_iota(jnp.int32, (places, spans), 0) == bucket
    pick = jnp.where(pick, 1.0, 0.0).astype(BF)
    rows[...] = jnp.zeros(rows.shape, F32)
    rows[:, pl.ds(0, SAMPLES)] = wave[...].astype(F32)
    lane = lax.broadcasted_iota(jnp.int32, (spans, 128), 1)
    tail = rows[:, pl.ds(256, 128)]
    tail = jnp.where(lane == SAMPLES - 256, column(slot) + 1.0, tail)
    tail = jnp.where(lane == SAMPLES - 255, column(length[...].astype(F32)) - 214.0, tail)
    rows[:, pl.ds(256, 128)] = tail
    packed = jnp.dot(pick, rows[...].astype(BF), preferred_element_type=F32)
    out[...] = packed.reshape(out.shape).astype(BF)


def gelu_parts(value):
    cumul = 0.5 * (1.0 + lax.erf(value * 0.7071067811865476))
    density = jnp.exp(-0.5 * value * value) * 0.3989422804014327
    return cumul, density


BLOCK = 16
BACK = 16
ROWS = 32 * BLOCK


def k_taps(conv0, weo):
    taps = jnp.concatenate([conv0[...].astype(F32), jnp.zeros((6, 512), F32)], axis=0).astype(BF)
    weo[...] = jnp.zeros(weo.shape, BF)
    weo[pl.ds(0, 16), pl.ds(0, 512)] = taps
    weo[pl.ds(16, 16), pl.ds(512, 512)] = taps


def tables(fold, window):
    sample = lax.broadcasted_iota(jnp.int32, (256, 128), 0).astype(F32)
    lane = lax.broadcasted_iota(jnp.int32, (256, 128), 1).astype(F32)
    tens = jnp.floor((sample + 0.5) * 0.1) * 10.0
    fold[pl.ds(0, 256), :] = jnp.where(sample - tens == lane, 1.0, 0.0).astype(BF)
    tens = jnp.floor((sample - 4.5) * 0.1) * 10.0
    odd = (sample >= 5.0) & (sample - 5.0 - tens + 16.0 == lane)
    fold[pl.ds(256, 256), :] = jnp.where(odd, 1.0, 0.0).astype(BF)
    step = lax.broadcasted_iota(jnp.int32, (32, 256), 0)
    step = jnp.where(step < 16, step, step - 16) * 10
    at = lax.broadcasted_iota(jnp.int32, (32, 256), 1)
    window[:, pl.ds(0, 256)] = jnp.where((at >= step) & (at < step + 10), 1.0, 0.0)
    window[:, pl.ds(256, 256)] = jnp.where((at >= step + 5) & (at < step + 15), 1.0, 0.0)


def tall(rows):
    return jnp.concatenate([rows] * 4, axis=0)


def dot_t(left, right):
    return lax.dot_general(left, right, (((0,), (0,)), ((), ())), preferred_element_type=F32)


def dot_nt(left, right):
    return lax.dot_general(left, right, (((1,), (1,)), ((), ())), preferred_element_type=F32)


def k_forward(
    scale, pos, arrived, weo, gain, bias, weight, fgrad,
    pre1, second_count, g, gs, se, so, ne, no, istd, valid, x, he, ho, other,
    fold, window, panels, am, pre, hs,
):
    spans = panels.shape[0]
    tables(fold, window)
    arr = arrived[...].astype(F32).reshape(128, WIDE).astype(BF)
    lane = lax.broadcasted_iota(jnp.int32, (128, 128), 1).astype(F32)
    meta = arr[:, 256:384].astype(F32)
    slot = meta[:, SAMPLES - 256 : SAMPLES - 255]
    place = jnp.where(slot - 1.0 == lane, 1.0, 0.0).astype(BF)
    moved = dot_t(place, arr)[0:spans]
    late = pltpu.roll(moved, WIDE - 160, 1)
    both = jnp.concatenate([moved[:, 0:256], late[:, 0:256]], axis=1)
    panels[...] = jnp.broadcast_to(both[:, None, :], panels.shape)
    length = moved[:, SAMPLES + 1 : SAMPLES + 2] + 214.0
    count = jnp.broadcast_to(jnp.floor((length - 9.5) * 0.2) + 1.0, (spans, 128))
    valid[...] = jnp.broadcast_to(count[:, None, :], valid.shape)
    second_count[...] = jnp.floor((count - 2.5) * 0.5) + 1.0
    frame = lax.broadcasted_iota(jnp.int32, (32, 128), 0).astype(F32)

    def block(b, carry):
        base = b * BLOCK

        def patch(q, carry):
            p = base + q
            count = tall(valid[p])
            keep_e, keep_o = 2.0 * frame < count, 2.0 * frame + 1.0 < count
            rows = pl.ds(pl.multiple_of(q * 32, 32), 32)
            for t in range(4):
                early = panels[p, :, pl.ds((t % 2) * 128, 128)]
                late = panels[p, :, pl.ds(256 + (t % 2) * 128, 128)]
                part = jnp.concatenate([early, early, late, late], axis=0)
                part = jnp.where(keep_e if t < 2 else keep_o, part * window[:, pl.ds(t * 128, 128)], 0.0)
                am[rows, pl.ds(t * 128, 128)] = part.astype(BF)
            return carry

        lax.fori_loop(0, BLOCK, patch, 0, unroll=BLOCK)
        every = pl.ds(pl.multiple_of(b * ROWS, ROWS), ROWS)
        xs = jnp.dot(am[...], fold[...], preferred_element_type=F32).astype(BF)
        x[every, :] = xs
        pre[...] = jnp.dot(xs, weo[...], preferred_element_type=F32)

        def norm(q, carry):
            p = base + q
            count = valid[p]
            inverse = 1.0 / count[0:1]
            wide = tall(count)
            keep_e, keep_o = 2.0 * frame < wide, 2.0 * frame + 1.0 < wide
            rows = pl.ds(pl.multiple_of(q * 32, 32), 32)
            at = pl.ds(pl.multiple_of(p * 32, 32), 32)
            for t in range(4):
                cols = pl.ds(t * 128, 128)
                e = pre[rows, cols]
                o = pre[rows, pl.ds(512 + t * 128, 128)]
                center = jnp.sum(e + o, axis=0, keepdims=True) * inverse
                e = jnp.where(keep_e, e - center, 0.0)
                o = jnp.where(keep_o, o - center, 0.0)
                variance = jnp.sum(e * e + o * o, axis=0, keepdims=True) * inverse
                rs = lax.rsqrt(variance + 1e-05)
                istd[p, :, cols] = jnp.broadcast_to(rs, (8, 128))
                scale_row, bias_row = gain[:, cols], bias[:, cols]
                for value, keep, n_ref, s_ref, h_ref in ((e, keep_e, ne, se, he), (o, keep_o, no, so, ho)):
                    value = value * rs
                    n_ref[at, cols] = value.astype(BF)
                    value = value * scale_row + bias_row
                    cumul, density = gelu_parts(value)
                    hidden = jnp.where(keep, value * cumul, 0.0)
                    s_ref[at, cols] = jnp.where(keep, cumul + value * density, 0.0).astype(BF)
                    h_ref[at, cols] = hidden.astype(BF)
                    if h_ref is he:
                        hs[rows, cols] = pltpu.roll(hidden, 31, 0).astype(BF)
            return carry

        lax.fori_loop(0, BLOCK, norm, 0, unroll=2)
        total = (
            jnp.dot(he[every, :], weight[0], preferred_element_type=F32)
            + jnp.dot(ho[every, :], weight[1], preferred_element_type=F32)
            + jnp.dot(hs[...], weight[2], preferred_element_type=F32)
        )
        for t in range(4):
            pre1[t, every, :] = total[:, t * 128 : t * 128 + 128]

        def second(q, carry):
            p = base + q
            count = tall(jnp.floor((valid[p] - 2.5) * 0.5) + 1.0)
            keep = frame < count
            at = pl.ds(pl.multiple_of(p * 32, 32), 32)
            for t in range(4):
                cols = pl.ds(t * 128, 128)
                value = pre1[t, at, :]
                cumul, density = gelu_parts(value)
                up = fgrad[p, :, cols].astype(F32) * scale
                up = jnp.concatenate([up, jnp.zeros((1, 128), F32)], axis=0)
                grad = jnp.where(keep, up * (cumul + value * density), 0.0)
                g[at, cols] = grad.astype(BF)
                gs[at, cols] = pltpu.roll(grad, 1, 0).astype(BF)
            return carry

        lax.fori_loop(0, BLOCK, second, 0, unroll=BLOCK)
        return carry

    lax.fori_loop(0, spans // BLOCK, block, 0, unroll=True)
    half_of(1 - pos[2], he, ho, g, gs, other)


def half_of(half, he, ho, g, gs, out):
    @pl.when(half == 0)
    def _():
        out[pl.ds(0, 512), :] = dot_t(he[...], g[...]).astype(out.dtype)
        out[pl.ds(512, 256), :] = dot_t(ho[:, pl.ds(0, 256)], g[...]).astype(out.dtype)

    @pl.when(half == 1)
    def _():
        out[pl.ds(0, 256), :] = dot_t(ho[:, pl.ds(256, 256)], g[...]).astype(out.dtype)
        out[pl.ds(256, 512), :] = dot_t(he[...], gs[...]).astype(out.dtype)


def k_half(pos, he, ho, g, gs, before, out):
    half_of(pos[2], he, ho, g, gs, out)


def k_features(pre1, count, before, feats, token):
    token[...] = jnp.zeros(token.shape, F32)
    spans = count.shape[0]

    def frame(t, carry):
        keep = count[...] > lax.convert_element_type(t, F32)
        for c in range(4):
            cols = pl.ds(c * 128, 128)
            value = pre1[c, pl.ds(t, spans, stride=32), :]
            cumul, _ = gelu_parts(value)
            feats[t, :, cols] = jnp.where(keep, value * cumul, 0.0).astype(BF)
        return carry

    lax.fori_loop(0, feats.shape[0], frame, 0, unroll=True)


def k_backward(
    first, g, gs, se, so, ne, no, istd, valid, x, gain, weight, start, before, small,
    de, do, dxe, dxo, sums,
):
    blocks = dxe.shape[0] // (32 * BACK)
    sums[...] = jnp.zeros(sums.shape, F32)

    def block(b, carry):
        base = (first + b) * BACK
        every = pl.ds(pl.multiple_of((first + b) * (32 * BACK), (32 * BACK)), (32 * BACK))
        de[...] = dot_nt(g[every, :], weight[0]) + dot_nt(gs[every, :], weight[2])
        do[...] = dot_nt(g[every, :], weight[1])

        def back(q, carry):
            p = base + q
            inverse = 1.0 / valid[p, pl.ds(0, 1), :]
            rows = pl.ds(pl.multiple_of(q * 32, 32), 32)
            at = pl.ds(pl.multiple_of(p * 32, 32), 32)
            here = pl.ds(pl.multiple_of((b * BACK + q) * 32, 32), 32)
            for t in range(4):
                cols = pl.ds(t * 128, 128)
                pe = de[rows, cols] * se[at, cols].astype(F32)
                po = do[rows, cols] * so[at, cols].astype(F32)
                e, o = ne[at, cols].astype(F32), no[at, cols].astype(F32)
                plain = jnp.sum(pe + po, axis=0, keepdims=True)
                mixed = jnp.sum(pe * e + po * o, axis=0, keepdims=True)
                sums[pl.ds(0, 1), cols] += mixed
                sums[pl.ds(1, 1), cols] += plain
                lead = istd[p, pl.ds(0, 1), cols] * gain[:, cols]
                plain, mixed = plain * inverse, mixed * inverse
                dxe[here, cols] = ((pe - plain - e * mixed) * lead).astype(BF)
                dxo[here, cols] = ((po - plain - o * mixed) * lead).astype(BF)
            return carry

        lax.fori_loop(0, BACK, back, 0, unroll=BACK)
        return carry

    lax.fori_loop(0, blocks, block, 0, unroll=True)
    part = x[pl.ds(first * (32 * BACK), blocks * (32 * BACK)), :]
    small[...] = start[...] + dot_t(part, dxe[...])[0:16] + dot_t(part, dxo[...])[16:32]
    small[pl.ds(10, 2), :] += sums[pl.ds(0, 2), :]


def encode(pos, arrived, conv0_weight, norm_gain, norm_bias, conv1_weight, feature_grad, scale):
    spans = feature_grad.shape[0]
    rows = spans * 32
    (weo,) = call(k_taps, [((128, 1024), BF)], [conv0_weight])
    gain, bias = norm_gain[None], norm_bias[None]
    wide = ((rows, 512), BF)
    pre1, count, g, gs, se, so, ne, no, istd, valid, x, he, ho, other = call(
        functools.partial(k_forward, scale),
        [
            ((4, rows, 128), F32), ((spans, 128), F32), wide, wide, wide, wide, wide, wide,
            ((spans, 8, 512), F32), ((spans, 8, 128), F32), ((rows, 128), BF), wide, wide, ((768, 512), BF),
        ],
        [arrived, weo, gain, bias, conv1_weight, feature_grad],
        pos,
        scratch=[
            ((512, 128), BF), ((32, 512), F32), ((spans, 8, 512), F32), ((ROWS, 512), BF), ((ROWS, 1024), F32),
            ((ROWS, 512), BF),
        ],
    )

    def features(before):
        frames = feature_grad.shape[1]
        return call(
            k_features, [((frames, spans, 512), BF), ((8, 128), F32)], [pre1, count], after=[before]
        )

    def mine(before):
        return call(k_half, [((768, 512), F32)], [he, ho, g, gs], pos, after=[before])[0]

    def backward(first, blocks, small, before):
        part, step = (32 * BACK * blocks, 512), (32 * BACK, 512)
        return call(
            functools.partial(k_backward, first),
            [((16, 512), F32)],
            [g, gs, se, so, ne, no, istd, valid, x, gain, conv1_weight, small],
            scratch=[(step, F32), (step, F32), (part, BF), (part, BF), ((8, 512), F32)],
            after=[before],
        )[0]

    return features, other, mine, backward


def body(waveform, lengths, target, conv0_weight, norm_gain, norm_bias, conv1_weight, feature_grad):
    spans = waveform.shape[1]
    devices = lax.axis_size("dp")
    frames = feature_grad.shape[2]
    pos = where_am_i()
    (packed,) = call(
        k_pack,
        [((devices, 2, WIDE), BF)],
        [],
        scratch=[
            ((spans, WIDE), F32), (waveform.shape[1:], BF), (lengths.shape, jnp.int32), (target.shape, jnp.int32),
            pltpu.SemaphoreType.DMA((3,)),
        ],
        after=[waveform[0], lengths, target],
        late=HBM,
        limit=60,
    )
    arrived = lax.all_to_all(packed, "dp", split_axis=0, concat_axis=0, tiled=True)
    scale = 1.0 / float(lax.axis_size("rep") * devices * spans * frames) ** 0.5
    features, other, mine, backward = encode(
        pos, arrived, conv0_weight, norm_gain, norm_bias, conv1_weight, feature_grad[0], scale
    )
    full, conv0, gain, bias, feats = reduce_all(pos, other, mine, backward, features)
    return (feats[None], conv0, gain, bias, full.reshape(conv1_weight.shape))


def solution(mesh):
    placed = (
        P("rep", "dp", None),
        P("rep", "dp"),
        P("rep", "dp"),
        P(),
        P(),
        P(),
        P(),
        P("rep", "dp", None, None),
    )
    return jax.shard_map(
        body,
        mesh=mesh,
        in_specs=placed,
        out_specs=(P("rep", "dp", None, None), P(), P(), P(), P()),
        check_vma=False,
    )
```
